32 devices in a mesh: grp: 2 (over y), space: 16 (over z, x, core).
Axes of the slice: x: 2, y: 2, z: 4, core: 2. Of those that a mesh axis runs over, the one named last changes fastest.
Arguments:
- gauge_links: bfloat16 [8, 2, 3, 3, 128, 2048], P('grp', None, None, None, None, 'space'), parts along dimension 0, may hold values from -2.5 to 2.5
- propagators: bfloat16 [4, 2, 4, 3, 128, 2048], P('grp', None, None, None, None, 'space'), parts along dimension 0, may hold values from -6 to 6
- sink_cotangent: bfloat16 [4, 2, 4, 3, 128, 2048], P('grp', None, None, None, 'space'), parts along dimension 0, may hold values from -6 to 6
- source_time: int32 [4], P('grp'), parts along dimension 0, may hold values from 0 to 7
- source_place: int32 [4, 3], P('grp'), parts along dimension 0, may hold values from 0 to 15
- pair_source: int32 [64], P('grp'), parts along dimension 0, may hold values from 0 to 1
- pair_separation: int32 [64], P('grp'), parts along dimension 0, may hold values from 0 to 7
- pair_owner: int32 [64, 1], P('grp'), parts along dimension 0, may hold values from 0 to 15; in each aligned block of 32 rows (0 to 31, 32 to 63, ...) at most 4 rows name the same one
Outputs:
- inserted: bfloat16 [4, 2, 4, 3, 128, 2048], P('grp', None, None, None, None, 'space'), parts along dimension 0
- correlator: float32 [128, 256], P(('grp', 'space')), parts along dimension 0
The draws below stay inside these ranges and needn't reach their ends.
There are 2 independent parts, one for each index of `grp`. The reference program is written for one: setup_inputs(seed, part) draws one part's arguments, and reference() takes and returns one part's arrays. A program takes and returns all parts, laid end to end along the dimension named above; each array names one. Nothing has to cross between parts.
Inputs may be any that keep to these rules, and one draw needn't show every extreme that they name: `pair_owner`: at most 4 pairs share an owner, and some owner has exactly 4.
All inputs are finite; a program needn't handle non-finite values.
Results may differ from the reference program's by a relative error of at most 0.0032.
Values may be sent and summed in bfloat16 or wider, within the bound.
No kernel may reach another device: no remote copies, remote signals or barrier semaphores. Data moves between devices by JAX's collectives and lax.ppermute only.
A program may use at most 256 MiB of HBM per device.

```python
import math
import jax
import jax.numpy as jnp
import numpy as np
from jax import lax

LT = 8
LX = 16
LY = 128
NSRC = 2
NMOM = 128
SLOTS = 4
TX = 128
LZ = 16
NPAIR = 32
OWNER_ROWS = 64
N_SPACE = 16


def with_ends(drawn, stream_key, low, top_value):
    shape = drawn.shape
    index_at = [jax.random.randint(jax.random.fold_in(stream_key, axis), (), 0, shape[axis]) for axis in range(len(shape))]
    drawn = drawn.at[tuple(index_at)].set(low)
    longest = shape.index(max(shape))
    index_at[longest] = (index_at[longest] + 1) % shape[longest]
    return drawn.at[tuple(index_at)].set(top_value)


def block_scale(own_key, shape, shards, smallest, high):
    loudness = 1.0
    for axis_at, parts in shards:
        heights = jax.random.uniform(jax.random.fold_in(jax.random.fold_in(own_key, 6), axis_at), (parts,), jnp.float32, smallest / len(shards), high / len(shards))
        loudness = loudness * jnp.repeat(jnp.exp(heights), shape[axis_at] // parts).reshape((-1,) + (1,) * (len(shape) - 1 - axis_at))
    return loudness


def assign_block(key, own, number, rows, number_of, top, most, lean):
    sequence = jax.random.permutation(key, number_of)
    packed, common = portions_of(number_of, rows * top, most, lean, True), portions_of(number_of, rows * top, most, lean, False)
    places = jnp.arange(number_of)

    def named(lengths, turn):
        used = int((lengths > 0).sum())
        fixed = max(1, used // 4)
        moved = fixed + (places - fixed + turn * (used - fixed)) % max(1, number_of - fixed)
        return jnp.zeros((number_of,), jnp.int32).at[sequence[jnp.where(places < fixed, places, moved)]].set(jnp.asarray(lengths, jnp.int32))

    lengths = jnp.where(number % 4 == 0, named(packed, number // 4), named(common, number - number // 4 - 1))
    mixed = jax.random.permutation(jax.random.fold_in(own, 3), number_of)
    donor, receiver = mixed[0:number_of // 2 * 2:2], mixed[1:number_of // 2 * 2:2]
    room = jnp.minimum(lengths[donor] - 1, most - lengths[receiver]) // 2
    room = jnp.where((donor == sequence[0]) | (receiver == sequence[0]) | (lengths[receiver] == 0), 0, jnp.maximum(room, 0))
    moved = jax.random.randint(jax.random.fold_in(own, 4), (number_of // 2,), 0, 1 << 20) % (room + 1)
    lengths = lengths.at[donor].add(-moved).at[receiver].add(moved)
    labels = jnp.searchsorted(jnp.cumsum(lengths), jnp.arange(rows * top), side="right").astype(jnp.int32)
    table = labels.reshape(top, rows).T
    table = table[jax.random.permutation(jax.random.fold_in(own, 1), rows)]
    turn = jax.random.randint(jax.random.fold_in(own, 2), (rows, 1), 0, top)
    return jnp.take_along_axis(table, (jnp.arange(top)[None, :] + turn) % top, axis=1)


def portions_of(number_of, total, reach, lean, full):
    loads = [(1 << 20) // math.isqrt(grade ** lean) + 1 for grade in range(1, number_of + 1)]
    largest = reach if full else min(reach, max(-(-total // number_of), total * loads[0] // sum(loads)))
    least = 1 if total - largest >= number_of - 1 else 0
    counts, rest = [largest] + [least] * (number_of - 1), total - largest - least * (number_of - 1)
    while rest > 0:
        free = [i for i in range(1, number_of) if counts[i] < largest] or [i for i in range(1, number_of) if counts[i] < reach]
        whole, left = sum([loads[i] for i in free]), rest
        for i in free:
            addition = min(reach - counts[i], max(1, left * loads[i] // whole), rest)
            counts[i] = counts[i] + addition
            rest = rest - addition
    return np.array(counts)


def gaussian(rng, shape, width, limit, cuts=(), kind=jnp.bfloat16):
    loudness = block_scale(rng, shape, cuts, -0.22, 0.18) if cuts else 1.0
    entries = jax.random.normal(rng, shape, jnp.float32) * width * loudness
    return jnp.minimum(jnp.maximum(entries, -limit), limit).astype(kind)


def setup_inputs(seed: int = 0, part: int = 0) -> dict:
    seeds = jax.random.split(jax.random.key(seed), 9)
    part_splits = jax.random.split(jax.random.fold_in(seeds[8], part), 9)
    gauge_links = gaussian(part_splits[0], (4, 2, 3, 3, TX, LZ * LY), 6 ** -0.5, 2.5, ((5, 16),))
    propagators = gaussian(part_splits[1], (NSRC, 2, 4, 3, TX, LZ * LY), 1.0, 6.0, ((5, 16),))
    sink_cotangent = gaussian(part_splits[2], (NSRC, 2, 4, 3, TX, LZ * LY), 1.0, 6.0, ((4, 16),))
    source_time = jax.random.randint(part_splits[3], (NSRC,), 0, LT).astype(jnp.int32)
    source_place = with_ends(jax.random.randint(part_splits[4], (NSRC, 3), 0, min(LX, LY)), jax.random.fold_in(part_splits[4], 1), 0, (min(LX, LY)) - 1).astype(jnp.int32)
    pair_source = with_ends(jax.random.randint(part_splits[5], (NPAIR,), 0, NSRC), jax.random.fold_in(part_splits[5], 1), 0, NSRC - 1).astype(jnp.int32)
    pair_separation = with_ends(jax.random.randint(part_splits[6], (NPAIR,), 0, LT), jax.random.fold_in(part_splits[6], 1), 0, LT - 1).astype(jnp.int32)
    pair_owner_keys = jax.random.split(jax.random.fold_in(part_splits[7], 1), NPAIR // NPAIR)
    pair_owner_turns = jax.random.permutation(jax.random.fold_in(part_splits[7], 3), NPAIR // NPAIR)
    pair_owner = jax.vmap(lambda own, number: assign_block(jax.random.fold_in(part_splits[7], 2), own, number, NPAIR, N_SPACE, 1, SLOTS, 2))(pair_owner_keys, pair_owner_turns).reshape((NPAIR, 1))
    return {"gauge_links": gauge_links, "propagators": propagators, "sink_cotangent": sink_cotangent, "source_time": source_time, "source_place": source_place, "pair_source": pair_source, "pair_separation": pair_separation, "pair_owner": pair_owner}


PLANES = ((0, 1), (0, 3), (1, 3), (0, 2), (1, 2), (3, 2))
OUTPUT_SCALE = 0.1

def sigma_tables():
    unit_imag = 1j
    gamma_x = np.array([[0, 0, 0, unit_imag], [0, 0, unit_imag, 0], [0, -unit_imag, 0, 0], [-unit_imag, 0, 0, 0]], dtype=complex)
    gamma_y = np.array([[0, 0, 0, -1], [0, 0, 1, 0], [0, 1, 0, 0], [-1, 0, 0, 0]], dtype=complex)
    gamma_z = np.array([[0, 0, unit_imag, 0], [0, 0, 0, -unit_imag], [-unit_imag, 0, 0, 0], [0, unit_imag, 0, 0]], dtype=complex)
    gamma_t = np.array([[0, 0, 1, 0], [0, 0, 0, 1], [1, 0, 0, 0], [0, 1, 0, 0]], dtype=complex)
    gammas = (gamma_x, gamma_y, gamma_z, gamma_t)
    tables = []
    for first_dir, second_dir in PLANES:
        tables.append(0.5 * (gammas[first_dir] @ gammas[second_dir] - gammas[second_dir] @ gammas[first_dir]))
    return tables

def complex_mul(left_pair, right_pair):
    left_re, left_im = left_pair
    right_re, right_im = right_pair
    rows_re = []
    rows_im = []
    for row in range(3):
        entry_re_list = []
        entry_im_list = []
        for col in range(3):
            acc_re = left_re[row, 0] * right_re[0, col] - left_im[row, 0] * right_im[0, col]
            acc_im = left_re[row, 0] * right_im[0, col] + left_im[row, 0] * right_re[0, col]
            for inner in (1, 2):
                acc_re = acc_re + left_re[row, inner] * right_re[inner, col] - left_im[row, inner] * right_im[inner, col]
                acc_im = acc_im + left_re[row, inner] * right_im[inner, col] + left_im[row, inner] * right_re[inner, col]
            entry_re_list.append(acc_re)
            entry_im_list.append(acc_im)
        rows_re.append(jnp.stack(entry_re_list))
        rows_im.append(jnp.stack(entry_im_list))
    return (jnp.stack(rows_re), jnp.stack(rows_im))

def adjoint(matrix_pair):
    return (jnp.swapaxes(matrix_pair[0], 0, 1), -jnp.swapaxes(matrix_pair[1], 0, 1))

def step_offset(direction, amount):
    result = [0, 0, 0, 0]
    result[direction] = amount
    return tuple(result)

def joined(first_offset, second_offset):
    return tuple((first_offset[index] + second_offset[index] for index in range(4)))

def clover_planes(fetch_link, fetch_staple):
    anchor = (0, 0, 0, 0)
    fields = []
    for first_dir, second_dir in PLANES:
        up_first = step_offset(first_dir, 1)
        down_first = step_offset(first_dir, -1)
        up_second = step_offset(second_dir, 1)
        down_second = step_offset(second_dir, -1)
        leaf_one = complex_mul(complex_mul(fetch_link(first_dir, anchor), fetch_link(second_dir, up_first)), complex_mul(adjoint(fetch_link(first_dir, up_second)), adjoint(fetch_link(second_dir, anchor))))
        leaf_two = complex_mul(complex_mul(fetch_link(second_dir, anchor), adjoint(fetch_link(first_dir, joined(up_second, down_first)))), complex_mul(adjoint(fetch_link(second_dir, down_first)), fetch_link(first_dir, down_first)))
        if second_dir == 2:
            leaf_three = complex_mul(adjoint(fetch_link(first_dir, down_first)), fetch_staple(first_dir, joined(down_first, down_second)))
            leaf_four = complex_mul(fetch_staple(first_dir, down_second), adjoint(fetch_link(first_dir, anchor)))
        else:
            diagonal_back = joined(down_first, down_second)
            leaf_three = complex_mul(complex_mul(adjoint(fetch_link(first_dir, down_first)), adjoint(fetch_link(second_dir, diagonal_back))), complex_mul(fetch_link(first_dir, diagonal_back), fetch_link(second_dir, down_second)))
            leaf_four = complex_mul(complex_mul(adjoint(fetch_link(second_dir, down_second)), fetch_link(first_dir, down_second)), complex_mul(fetch_link(second_dir, joined(down_second, up_first)), adjoint(fetch_link(first_dir, anchor))))
        total_re = leaf_one[0] + leaf_two[0] + leaf_three[0] + leaf_four[0]
        total_im = leaf_one[1] + leaf_two[1] + leaf_three[1] + leaf_four[1]
        anti_re = (total_re - jnp.swapaxes(total_re, 0, 1)) / 8.0
        anti_im = (total_im + jnp.swapaxes(total_im, 0, 1)) / 8.0
        trace_third = (anti_im[0, 0] + anti_im[1, 1] + anti_im[2, 2]) / 3.0
        identity = jnp.eye(3, dtype=jnp.float32).reshape((3, 3) + (1,) * (anti_im.ndim - 2))
        fields.append((anti_re, anti_im - identity * trace_third))
    return fields

def insert_field(fields, spinor_re, spinor_im):
    tables = sigma_tables()
    rows_re = [0.0, 0.0, 0.0, 0.0]
    rows_im = [0.0, 0.0, 0.0, 0.0]
    for plane_index in range(6):
        field_re, field_im = fields[plane_index]
        mixed_re = 0.0
        mixed_im = 0.0
        for column in range(3):
            coef_re = field_re[:, column]
            coef_im = field_im[:, column]
            vector_re = spinor_re[:, :, column:column + 1]
            vector_im = spinor_im[:, :, column:column + 1]
            mixed_re = mixed_re + coef_re * vector_re - coef_im * vector_im
            mixed_im = mixed_im + coef_re * vector_im + coef_im * vector_re
        sigma_table = tables[plane_index]
        for spin_row in range(4):
            for spin_col in range(4):
                table_entry = sigma_table[spin_row, spin_col]
                if abs(table_entry) > 0:
                    entry_re = float(table_entry.real)
                    entry_im = float(table_entry.imag)
                    rows_re[spin_row] = rows_re[spin_row] + entry_re * mixed_re[:, spin_col] - entry_im * mixed_im[:, spin_col]
                    rows_im[spin_row] = rows_im[spin_row] + entry_re * mixed_im[:, spin_col] + entry_im * mixed_re[:, spin_col]
    return (jnp.stack(rows_re, axis=1), jnp.stack(rows_im, axis=1))

def triple_density(inserted_pair, plain_pair, sink_pair):
    ins_re, ins_im = inserted_pair
    plain_re, plain_im = plain_pair
    sink_re, sink_im = sink_pair
    total_re = 0.0
    total_im = 0.0
    for color_index, left_color, right_color in ((0, 1, 2), (1, 2, 0), (2, 0, 1)):
        cross_re = plain_re[:, :, left_color] * sink_re[:, :, right_color] - plain_im[:, :, left_color] * sink_im[:, :, right_color] - plain_re[:, :, right_color] * sink_re[:, :, left_color] + plain_im[:, :, right_color] * sink_im[:, :, left_color]
        cross_im = plain_re[:, :, left_color] * sink_im[:, :, right_color] + plain_im[:, :, left_color] * sink_re[:, :, right_color] - plain_re[:, :, right_color] * sink_im[:, :, left_color] - plain_im[:, :, right_color] * sink_re[:, :, left_color]
        total_re = total_re + lax.optimization_barrier(jnp.sum(ins_re[:, :, color_index] * cross_re - ins_im[:, :, color_index] * cross_im, axis=1))
        total_im = total_im + lax.optimization_barrier(jnp.sum(ins_re[:, :, color_index] * cross_im + ins_im[:, :, color_index] * cross_re, axis=1))
    return (total_re, total_im)

def momentum_numbers(count):
    index_list = jnp.arange(count, dtype=jnp.int32)
    return (index_list % 4 - 1, index_list // 4 % 4 - 1, index_list // 16 - count // 32)

def phase_fraction(waves, coords, extent_z):
    wave_x, wave_y, wave_z = waves
    coord_x, coord_y, coord_z = coords
    return (wave_x * coord_x % LX).astype(jnp.float32) / LX + (wave_y * coord_y % LY).astype(jnp.float32) / LY + (wave_z * coord_z % extent_z).astype(jnp.float32) / extent_z

def project(density_re, density_im, z_positions, extent_z):
    source_count = density_re.shape[0]
    flat_re = density_re.reshape((source_count * LT, -1))
    flat_im = density_im.reshape((source_count * LT, -1))
    wave_x, wave_y, wave_z = momentum_numbers(NMOM)
    waves = (wave_x[None, None, None, :], wave_y[None, None, None, :], wave_z[None, None, None, :])
    coords = (jnp.arange(LX, dtype=jnp.int32)[:, None, None, None], jnp.arange(LY, dtype=jnp.int32)[None, None, :, None], z_positions[None, :, None, None])
    phase_angle = (2.0 * math.pi * phase_fraction(waves, coords, extent_z)).reshape((-1, NMOM))
    cos_table = jnp.cos(phase_angle)
    sin_table = jnp.sin(phase_angle)
    highest = lax.Precision.HIGHEST
    out_re = jnp.dot(flat_re, cos_table, precision=highest) + jnp.dot(flat_im, sin_table, precision=highest)
    out_im = jnp.dot(flat_im, cos_table, precision=highest) - jnp.dot(flat_re, sin_table, precision=highest)
    return (out_re, out_im)

def owner_rows(projected_re, projected_im, source_time, source_place, pair_source, pair_separation, pair_owner, extent_z, row_count):
    highest = lax.Precision.HIGHEST
    source_count = source_time.shape[0]
    pair_count = pair_source.shape[0]
    source_hits = (pair_source[:, None] == jnp.arange(source_count, dtype=jnp.int32)[None, :]).astype(jnp.int32)
    start_time = lax.optimization_barrier(jnp.sum(source_hits * source_time[None, :], axis=1))
    slice_time = (start_time + pair_separation) % LT
    chosen = pair_source * LT + slice_time
    selector = (chosen[:, None] == jnp.arange(source_count * LT, dtype=jnp.int32)[None, :]).astype(jnp.float32)
    picked_re = jnp.dot(selector, projected_re, precision=highest)
    picked_im = jnp.dot(selector, projected_im, precision=highest)
    position = lax.optimization_barrier(jnp.sum(source_hits[:, :, None] * source_place[None, :, :], axis=1))
    wave_x, wave_y, wave_z = momentum_numbers(projected_re.shape[1])
    waves = (wave_x[None, :], wave_y[None, :], wave_z[None, :])
    coords = (position[:, 0:1], position[:, 1:2], position[:, 2:3])
    phase_angle = 2.0 * math.pi * phase_fraction(waves, coords, extent_z)
    cos_part = jnp.cos(phase_angle)
    sin_part = jnp.sin(phase_angle)
    turned_re = picked_re * cos_part - picked_im * sin_part
    turned_im = picked_re * sin_part + picked_im * cos_part
    values = jnp.concatenate([turned_re, turned_im], axis=1) * (OUTPUT_SCALE / math.sqrt(LX * LY * extent_z))
    owner_index = pair_owner[:, 0]
    pair_index = jnp.arange(pair_count, dtype=jnp.int32)
    earlier = (owner_index[:, None] == owner_index[None, :]) & (pair_index[None, :] < pair_index[:, None])
    slot_index = lax.optimization_barrier(jnp.sum(earlier.astype(jnp.int32), axis=1))
    target = owner_index * SLOTS + slot_index
    placer = (jnp.arange(row_count, dtype=jnp.int32)[:, None] == target[None, :]).astype(jnp.float32)
    return jnp.dot(placer, values, precision=highest)

def reference(gauge_links, propagators, sink_cotangent, source_time, source_place, pair_source, pair_separation, pair_owner):
    links_grid = gauge_links.reshape((4, 2, 3, 3, LT, LX, LZ, LY))

    def lattice_shift(field, offset):
        return jnp.roll(field, (-offset[3], -offset[0], -offset[2], -offset[1]), axis=(-4, -3, -2, -1))

    def fetch_link(direction, offset):
        moved_field = lattice_shift(links_grid[direction], offset)
        return (moved_field[0].astype(jnp.float32), moved_field[1].astype(jnp.float32))
    anchor = (0, 0, 0, 0)
    staples = []
    for direction in (0, 1, 3):
        staple = complex_mul(complex_mul(adjoint(fetch_link(2, anchor)), fetch_link(direction, anchor)), fetch_link(2, step_offset(direction, 1)))
        staples.append(lax.optimization_barrier(jnp.stack(staple).astype(jnp.bfloat16)))

    def fetch_staple(direction, offset):
        moved_field = lattice_shift(staples[min(direction, 2)], offset)
        return (moved_field[0].astype(jnp.float32), moved_field[1].astype(jnp.float32))
    fields = clover_planes(fetch_link, fetch_staple)
    spinor_grid = propagators.reshape((NSRC, 2, 4, 3, LT, LX, LZ, LY))
    sink_grid = sink_cotangent.reshape((NSRC, 2, 4, 3, LT, LX, LZ, LY))
    inserted_blocks = []
    density_re_list = []
    density_im_list = []
    for source_index in range(NSRC):
        plain_block = spinor_grid[source_index:source_index + 1].astype(jnp.float32)
        ins_re, ins_im = insert_field(fields, plain_block[:, 0], plain_block[:, 1])
        inserted_block = lax.optimization_barrier(jnp.stack([ins_re, ins_im], axis=1).astype(jnp.bfloat16))
        inserted_blocks.append(inserted_block)
        inserted_wide = inserted_block.astype(jnp.float32)
        sink_block = sink_grid[source_index:source_index + 1].astype(jnp.float32)
        density_re, density_im = triple_density((inserted_wide[:, 0], inserted_wide[:, 1]), (plain_block[:, 0], plain_block[:, 1]), (sink_block[:, 0], sink_block[:, 1]))
        density_re_list.append(density_re)
        density_im_list.append(density_im)
    inserted = jnp.concatenate(inserted_blocks, axis=0).reshape(propagators.shape)
    density_re = jnp.concatenate(density_re_list, axis=0)
    density_im = jnp.concatenate(density_im_list, axis=0)
    projected_re, projected_im = project(density_re, density_im, jnp.arange(LZ, dtype=jnp.int32), LZ)
    correlator = owner_rows(projected_re, projected_im, source_time, source_place, pair_source, pair_separation, pair_owner, LZ, OWNER_ROWS)
    return (inserted, correlator)
```

```python
import functools
import math

import jax
import jax.numpy as jnp
import numpy as np
from jax import lax
from jax.experimental import pallas as pl
from jax.experimental.pallas import tpu as pltpu
from jax.sharding import PartitionSpec as P

LT = 8
LX = 16
LY = 128
TX = LT * LX
NMOM = 128
SLOTS = 4
OUTPUT_SCALE = 0.1
F32 = jnp.float32
BF16 = jnp.bfloat16
VMEM_BYTES = 56 * 1024 * 1024
UPPER = ((0, 1), (0, 2), (1, 2))
SYMMETRIC = ((0, 0), (1, 1), (2, 2), (0, 1), (0, 2), (1, 2))
HALF = len(UPPER) + len(SYMMETRIC)


def from_behind(block, distance):
    count = lax.axis_size("space")
    return lax.ppermute(block, "space", [((i - distance) % count, i) for i in range(count)])


def entry(left, right, row, col, left_dagger, right_dagger, part):
    total = None
    for inner in range(3):
        a_re, a_im = left[inner][row] if left_dagger else left[row][inner]
        b_re, b_im = right[col][inner] if right_dagger else right[inner][col]
        if part == 0:
            first, second = a_re * b_re, a_im * b_im
            negative = left_dagger == right_dagger
        elif left_dagger:
            first, second = a_re * b_im, a_im * b_re
            negative = True
        else:
            first, second = a_im * b_re, a_re * b_im
            negative = right_dagger
        total = first if total is None else total + first
        total = total - second if negative else total + second
    return total


def product(left, right, left_dagger=False, right_dagger=False):
    return [
        [
            tuple(entry(left, right, i, j, left_dagger, right_dagger, part) for part in (0, 1))
            for j in range(3)
        ]
        for i in range(3)
    ]


def anti_product(left, right):
    kept = []
    for i, j in UPPER:
        kept.append(entry(left, right, i, j, False, False, 0) - entry(left, right, j, i, False, False, 0))
    for i, j in SYMMETRIC:
        value = entry(left, right, i, j, False, False, 1)
        kept.append(value + (value if i == j else entry(left, right, j, i, False, False, 1)))
    return kept


def minus_adjoint(left, right):
    return [
        [
            (left[i][j][0] - right[j][i][0], left[i][j][1] + right[j][i][1])
            for j in range(3)
        ]
        for i in range(3)
    ]


def mapped(function, matrix):
    return [[tuple(function(part) for part in item) for item in row] for row in matrix]


def rows_of(time):
    return pl.ds(pl.multiple_of(time * LX, LX), LX)


def next_time(time):
    return lax.rem(time + 1, LT)


def last_time(time):
    return lax.rem(time + LT - 1, LT)


def load_matrix(ref, direction, time):
    rows = rows_of(time)
    return [
        [tuple(ref[direction, part, i, j, rows, :].astype(F32) for part in (0, 1)) for j in range(3)]
        for i in range(3)
    ]


def up_x(value):
    return pltpu.roll(value, LX - 1, 0)


def down_x(value):
    return pltpu.roll(value, 1, 0)


def up_y(value):
    return pltpu.roll(value, LY - 1, 1)


def down_y(value):
    return pltpu.roll(value, 1, 1)


def neighbour_link(ref, direction, step, time):
    if step == 3:
        return load_matrix(ref, direction, next_time(time))
    return mapped(up_x if step == 0 else up_y, load_matrix(ref, direction, time))


def staple_kernel(links, out):
    def body(time, carry):
        rows = rows_of(time)
        up_link = load_matrix(links, 2, time)
        for slot, direction in enumerate((0, 1, 3)):
            left = product(up_link, load_matrix(links, direction, time), left_dagger=True)
            staple = product(left, neighbour_link(links, 2, direction, time))
            for i in range(3):
                for j in range(3):
                    for part in (0, 1):
                        out[slot, part, i, j, rows, :] = staple[i][j][part].astype(BF16)
        return carry

    lax.fori_loop(0, LT, body, 0)


def flat_kernel(links, out, corner):
    def lower(time, carry):
        rows = rows_of(time)
        for slot, direction in enumerate((0, 1)):
            bent = product(
                load_matrix(links, direction, time), neighbour_link(links, 3, direction, time)
            )
            bent = product(load_matrix(links, 3, time), bent, left_dagger=True)
            for i in range(3):
                for j in range(3):
                    for part in (0, 1):
                        corner[slot, part, i, j, rows, :] = bent[i][j][part]
        return carry

    lax.fori_loop(0, LT, lower, 0)

    def upper(time, carry):
        rows = rows_of(time)
        for slot, direction in enumerate((0, 1)):
            far = product(
                load_matrix(links, 3, time), neighbour_link(links, direction, 3, time)
            )
            far = product(neighbour_link(links, 3, direction, time), far, right_dagger=True)
            bend = minus_adjoint(far, load_matrix(corner, slot, last_time(time)))
            link = load_matrix(links, direction, time)
            ahead = anti_product(link, bend)
            behind = anti_product(bend, link)
            move = down_x if direction == 0 else down_y
            for index in range(HALF):
                out[(slot + 1) * HALF + index, rows, :] = ahead[index] + move(behind[index])
        link_x, link_y = load_matrix(links, 0, time), load_matrix(links, 1, time)
        over_x, over_y = mapped(up_y, link_x), mapped(up_x, link_y)
        near = product(link_x, product(link_y, over_x), left_dagger=True)
        far = product(over_x, product(link_x, over_y), right_dagger=True)
        bend = minus_adjoint(far, mapped(down_x, near))
        ahead = anti_product(link_y, bend)
        behind = anti_product(bend, link_y)
        for index in range(HALF):
            out[index, rows, :] = -(ahead[index] + down_y(behind[index]))
        return carry

    lax.fori_loop(0, LT, upper, 0)


def insert_kernel(links, above, staples, flat, plain, inserted, crossed, rise, behind_t):
    def planes(time, carry):
        rows = rows_of(time)
        up_link = load_matrix(links, 2, time)
        for slot, direction in enumerate((0, 1, 3)):
            far = product(up_link, load_matrix(above, slot, time))
            far = product(neighbour_link(links, 2, direction, time), far, right_dagger=True)
            bend = minus_adjoint(far, load_matrix(staples, slot, time))
            link = load_matrix(links, direction, time)
            ahead = anti_product(link, bend)
            behind = anti_product(bend, link)
            for index in range(HALF):
                if direction == 3:
                    rise[slot * HALF + index, rows, :] = ahead[index]
                    behind_t[index, rows, :] = behind[index]
                else:
                    move = down_x if direction == 0 else down_y
                    rise[slot * HALF + index, rows, :] = ahead[index] + move(behind[index])
        return carry

    lax.fori_loop(0, LT, planes, 0)

    def insertion(time, carry):
        rows = rows_of(time)
        before = rows_of(last_time(time))
        for block in range(2):
            sign = 1.0 if block == 0 else -1.0

            def field(number):
                parts = []
                for index in range(HALF):
                    if number == 0:
                        value = sign * flat[HALF + index, rows, :] - rise[HALF + index, rows, :]
                    elif number == 1:
                        value = -sign * flat[2 * HALF + index, rows, :] - rise[index, rows, :]
                    else:
                        last = rise[2 * HALF + index, rows, :] + behind_t[index, before, :]
                        value = -flat[index, rows, :] - sign * last
                    parts.append(value * 0.125)
                trace = (parts[3] + parts[4] + parts[5]) * (1.0 / 3.0)
                for index in (3, 4, 5):
                    parts[index] = parts[index] - trace
                matrix = [[None] * 3 for _ in range(3)]
                for index, (i, j) in enumerate(UPPER):
                    re, im = parts[index], parts[6 + index]
                    matrix[i][j] = (re, im)
                    matrix[j][i] = (-re, im)
                for i in range(3):
                    matrix[i][i] = (None, parts[3 + i])
                return matrix

            first, second, third = field(0), field(1), field(2)
            same = [
                [(-third[i][j][1], None if i == j else third[i][j][0]) for j in range(3)]
                for i in range(3)
            ]
            cross = [
                [
                    (
                        -first[i][j][1] if i == j else second[i][j][0] - first[i][j][1],
                        second[i][j][1] if i == j else first[i][j][0] + second[i][j][1],
                    )
                    for j in range(3)
                ]
                for i in range(3)
            ]
            for source in range(plain.shape[0]):
                spinor = [
                    [
                        tuple(
                            plain[source, part, 2 * block + spin, color, rows, :].astype(F32)
                            for part in (0, 1)
                        )
                        for color in range(3)
                    ]
                    for spin in range(2)
                ]
                for spin in range(2):
                    result = []
                    for i in range(3):
                        total_re = total_im = None
                        for j in range(3):
                            m_re, m_im = same[i][j]
                            v_re, v_im = spinor[spin][j]
                            re, im = m_re * v_re, m_re * v_im
                            if m_im is not None:
                                re, im = re - m_im * v_im, im + m_im * v_re
                            if spin == 0:
                                total_re = re if total_re is None else total_re + re
                                total_im = im if total_im is None else total_im + im
                            else:
                                total_re = -re if total_re is None else total_re - re
                                total_im = -im if total_im is None else total_im - im
                        for j in range(3):
                            v_re, v_im = spinor[1 - spin][j]
                            if spin == 0:
                                m_re, m_im = cross[i][j]
                                total_re = total_re + m_re * v_re - m_im * v_im
                                total_im = total_im + m_re * v_im + m_im * v_re
                            else:
                                m_re, m_im = cross[j][i]
                                total_re = total_re + m_re * v_re + m_im * v_im
                                total_im = total_im + m_re * v_im - m_im * v_re
                        kept = (total_re.astype(BF16), total_im.astype(BF16))
                        for part in (0, 1):
                            inserted[source, part, 2 * block + spin, i, rows, :] = kept[part]
                        result.append(tuple(part.astype(F32) for part in kept))
                    for a, b, c in ((0, 1, 2), (1, 2, 0), (2, 0, 1)):
                        a_re, a_im = result[a]
                        b_re, b_im = result[b]
                        p_re, p_im = spinor[spin][a]
                        q_re, q_im = spinor[spin][b]
                        crossed[source, 0, 2 * block + spin, c, rows, :] = (
                            a_re * q_re - a_im * q_im - b_re * p_re + b_im * p_im
                        )
                        crossed[source, 1, 2 * block + spin, c, rows, :] = (
                            a_re * q_im + a_im * q_re - b_re * p_im - b_im * p_re
                        )
        return carry

    lax.fori_loop(0, LT, insertion, 0)


def project_kernel(sources, crossed, sink, wave_y, wave_x, turn, owner, out, density):
    count = sources * LT * LX

    def body(time, carry):
        rows = rows_of(time)
        for source in range(sources):
            total_re = total_im = None
            for spin in range(4):
                for color in range(3):
                    eta = []
                    for part in (0, 1):
                        line = (((source * 2 + part) * 4) + spin) * 3 + color
                        eta.append(
                            jnp.concatenate(
                                [sink[2 * time + half, pl.ds(line * 8, 8), :] for half in (0, 1)],
                                axis=0,
                            ).astype(F32)
                        )
                    w_re = crossed[source, 0, spin, color, rows, :]
                    w_im = crossed[source, 1, spin, color, rows, :]
                    re = w_re * eta[0] - w_im * eta[1]
                    im = w_re * eta[1] + w_im * eta[0]
                    total_re = re if total_re is None else total_re + re
                    total_im = im if total_im is None else total_im + im
            place = pl.multiple_of(source * TX + time * LX, LX)
            density[pl.ds(place, LX), :] = total_re
            density[pl.ds(pl.multiple_of(count + place, LX), LX), :] = total_im
        return carry

    lax.fori_loop(0, LT, body, 0)
    values = density[...]
    high = values.astype(BF16)
    low = (values - high.astype(F32)).astype(BF16)
    both = functools.partial(jnp.dot, preferred_element_type=F32)
    waves = both(high, wave_y[0]) + (both(low, wave_y[0]) + both(high, wave_y[1]))
    cos_re, sin_re = waves[:count, :NMOM], waves[:count, NMOM:]
    cos_im, sin_im = waves[count:, :NMOM], waves[count:, NMOM:]
    line_re = (cos_re + sin_im).reshape(sources * LT, LX, NMOM)
    line_im = (cos_im - sin_re).reshape(sources * LT, LX, NMOM)
    cos_x, sin_x = wave_x[0][None], wave_x[1][None]
    sum_re = jnp.sum(line_re * cos_x + line_im * sin_x, axis=1)
    sum_im = jnp.sum(line_im * cos_x - line_re * sin_x, axis=1)
    cos_t, sin_t = turn[0], turn[1]
    turned = jnp.concatenate(
        [sum_re * cos_t - sum_im * sin_t, sum_re * sin_t + sum_im * cos_t], axis=1
    )
    out[...] = jnp.dot(
        owner[...], turned, precision=lax.Precision.HIGHEST, preferred_element_type=F32
    )


def spread_kernel(sink, out):
    for device in range(out.shape[0]):
        piece = sink[:, :, device * LY : (device + 1) * LY].astype(F32)
        out[device] = piece.reshape(out.shape[1], LY).astype(BF16)


def params():
    return pltpu.CompilerParams(vmem_limit_bytes=VMEM_BYTES)


def whole(count):
    return [pl.BlockSpec(memory_space=pltpu.VMEM)] * count


def cost(flops, moved):
    return pl.CostEstimate(flops=flops, bytes_accessed=moved, transcendentals=0)


def momenta():
    index = np.arange(NMOM)
    return index % 4 - 1, index // 4 % 4 - 1, index // 16 - NMOM // 32


def wave_tables():
    wave_x, wave_y, _ = momenta()
    angle_y = 2.0 * np.pi * ((wave_y[None, :] * np.arange(LY)[:, None]) % LY) / LY
    table = np.concatenate([np.cos(angle_y), np.sin(angle_y)], axis=1)
    high = table.astype(jnp.bfloat16)
    low = (table - high.astype(np.float64)).astype(jnp.bfloat16)
    angle_x = 2.0 * np.pi * ((wave_x[None, :] * np.arange(LX)[:, None]) % LX) / LX
    along_x = np.stack([np.cos(angle_x), np.sin(angle_x)]).astype(np.float32)
    return np.stack([high, low]), along_x


def turn_table(source_place, z_position, extent_z):
    wave_x, wave_y, wave_z = (jnp.asarray(w, jnp.int32)[None, :] for w in momenta())
    fraction = (
        (wave_x * source_place[:, 0:1] % LX).astype(F32) / LX
        + (wave_y * source_place[:, 1:2] % LY).astype(F32) / LY
        + (wave_z * (source_place[:, 2:3] - z_position) % extent_z).astype(F32) / extent_z
    )
    angle = 2.0 * math.pi * fraction
    scale = OUTPUT_SCALE / math.sqrt(LX * LY * extent_z)
    table = jnp.stack([jnp.cos(angle), jnp.sin(angle)]) * scale
    return jnp.repeat(table, LT, axis=1)


def owner_table(source_time, pair_source, pair_separation, pair_owner, row_count):
    sources = source_time.shape[0]
    pairs = pair_source.shape[0]
    hits = pair_source[:, None] == jnp.arange(sources, dtype=jnp.int32)[None, :]
    start = jnp.sum(jnp.where(hits, source_time[None, :], 0), axis=1)
    chosen = pair_source * LT + (start + pair_separation) % LT
    picks = chosen[:, None] == jnp.arange(sources * LT, dtype=jnp.int32)[None, :]
    owner = pair_owner[:, 0]
    number = jnp.arange(pairs, dtype=jnp.int32)
    earlier = (owner[:, None] == owner[None, :]) & (number[None, :] < number[:, None])
    target = owner * SLOTS + jnp.sum(earlier.astype(jnp.int32), axis=1)
    rows = jnp.arange(row_count, dtype=jnp.int32)[:, None] == target[None, :]
    return jnp.dot(rows.astype(BF16), picks.astype(BF16), preferred_element_type=F32)


def on_device(
    gauge_links,
    propagators,
    sink_cotangent,
    source_time,
    source_place,
    pair_source,
    pair_separation,
    pair_owner,
):
    devices = lax.axis_size("space")
    assert gauge_links.shape[5] == LY
    sources = propagators.shape[0]
    lines = sources * 2 * 4 * 3
    slab = TX // devices
    site = (TX, LY)

    above = jnp.concatenate(
        [from_behind(gauge_links[0:2], -1), from_behind(gauge_links[3:4], -1)], axis=0
    )
    own_staples = pl.pallas_call(
        staple_kernel,
        out_shape=jax.ShapeDtypeStruct((3, 2, 3, 3) + site, BF16),
        in_specs=whole(1),
        out_specs=whole(1)[0],
        compiler_params=params(),
        cost_estimate=cost(6 * 216 * TX * LY, 4 << 20),
        name="staples",
    )(gauge_links)
    staples = from_behind(own_staples, 1)

    if slab == 8:
        spread = pl.pallas_call(
            spread_kernel,
            out_shape=jax.ShapeDtypeStruct((devices, lines * slab, LY), BF16),
            in_specs=whole(1),
            out_specs=whole(1)[0],
            compiler_params=params(),
            cost_estimate=cost(lines * TX * LY, 3 << 20),
            name="spread",
        )(sink_cotangent.reshape(lines, slab, devices * LY))
    else:
        spread = (
            sink_cotangent.reshape(lines, slab, devices, LY)
            .transpose(2, 0, 1, 3)
            .reshape(devices, lines * slab, LY)
        )
    sink = lax.all_to_all(spread, "space", split_axis=0, concat_axis=0, tiled=True)
    if slab != 8:
        sink = (
            sink.reshape(TX // 8, 8 // slab, lines, slab, LY)
            .transpose(0, 2, 1, 3, 4)
            .reshape(TX // 8, lines * 8, LY)
        )

    flat = pl.pallas_call(
        flat_kernel,
        out_shape=jax.ShapeDtypeStruct((3 * HALF,) + site, F32),
        in_specs=whole(1),
        out_specs=whole(1)[0],
        scratch_shapes=[pltpu.VMEM((2, 2, 3, 3) + site, F32)],
        compiler_params=params(),
        cost_estimate=cost(18 * 200 * TX * LY, 4 << 20),
        name="flat_planes",
    )(gauge_links)

    inserted, crossed = pl.pallas_call(
        insert_kernel,
        out_shape=(
            jax.ShapeDtypeStruct(propagators.shape, BF16),
            jax.ShapeDtypeStruct(propagators.shape, F32),
        ),
        in_specs=whole(5),
        out_specs=tuple(whole(2)),
        scratch_shapes=[pltpu.VMEM((3 * HALF,) + site, F32), pltpu.VMEM((HALF,) + site, F32)],
        compiler_params=params(),
        cost_estimate=cost(5000 * TX * LY, 12 << 20),
        name="insertion",
    )(gauge_links, above, staples, flat, propagators)

    table_y, table_x = wave_tables()
    turn = turn_table(source_place, lax.axis_index("space"), devices)
    owner = owner_table(
        source_time, pair_source, pair_separation, pair_owner, devices * SLOTS
    )
    rows = pl.pallas_call(
        functools.partial(project_kernel, sources),
        out_shape=jax.ShapeDtypeStruct((devices * SLOTS, 2 * NMOM), F32),
        in_specs=whole(6),
        out_specs=whole(1)[0],
        scratch_shapes=[pltpu.VMEM((2 * sources * TX, LY), F32)],
        compiler_params=params(),
        cost_estimate=cost(300 * TX * LY, 5 << 20),
        name="projection",
    )(crossed, sink, jnp.asarray(table_y), jnp.asarray(table_x), turn, owner)
    parts = lax.all_to_all(
        rows.reshape(devices, SLOTS, 2 * NMOM), "space", split_axis=0, concat_axis=0, tiled=True
    )
    return inserted, jnp.sum(parts, axis=0)


def solution(mesh):
    placed = (
        P("grp", None, None, None, None, "space"),
        P("grp", None, None, None, None, "space"),
        P("grp", None, None, None, "space", None),
        P("grp"),
        P("grp", None),
        P("grp"),
        P("grp"),
        P("grp", None),
    )
    return jax.shard_map(
        on_device,
        mesh=mesh,
        in_specs=placed,
        out_specs=(P("grp", None, None, None, None, "space"), P(("grp", "space"), None)),
        check_vma=False,
    )
```

```python
import functools
import math

import jax
import jax.numpy as jnp
import numpy as np
from jax import lax
from jax.experimental import pallas as pl
from jax.experimental.pallas import tpu as pltpu
from jax.sharding import PartitionSpec as P

LT = 8
LX = 16
LY = 128
TX = LT * LX
NMOM = 128
SLOTS = 4
OUTPUT_SCALE = 0.1
F32 = jnp.float32
BF16 = jnp.bfloat16
PIECES = ((0, 4), (4, 8))
PADDED = 8
UPPER = ((0, 1), (0, 2), (1, 2))
SYMMETRIC = ((0, 0), (1, 1), (2, 2), (0, 1), (0, 2), (1, 2))
HALVES = (slice(0, 8), slice(8, 16))
HALF = len(UPPER) + len(SYMMETRIC)


def from_behind(block, distance):
    count = lax.axis_size("space")
    return lax.ppermute(block, "space", [((i - distance) % count, i) for i in range(count)])


def entry(left, right, row, col, left_dagger, right_dagger, part):
    total = None
    for inner in range(3):
        a_re, a_im = left[inner][row] if left_dagger else left[row][inner]
        b_re, b_im = right[col][inner] if right_dagger else right[inner][col]
        if part == 0:
            first, second = a_re * b_re, a_im * b_im
            negative = left_dagger == right_dagger
        elif left_dagger:
            first, second = a_re * b_im, a_im * b_re
            negative = True
        else:
            first, second = a_im * b_re, a_re * b_im
            negative = right_dagger
        total = first if total is None else total + first
        total = total - second if negative else total + second
    return total


def product(left, right, left_dagger=False, right_dagger=False):
    return [
        [
            tuple(entry(left, right, i, j, left_dagger, right_dagger, part) for part in (0, 1))
            for j in range(3)
        ]
        for i in range(3)
    ]


def anti_product(left, right):
    kept = []
    for i, j in UPPER:
        kept.append(entry(left, right, i, j, False, False, 0) - entry(left, right, j, i, False, False, 0))
    for i, j in SYMMETRIC:
        value = entry(left, right, i, j, False, False, 1)
        kept.append(value + (value if i == j else entry(left, right, j, i, False, False, 1)))
    return kept


def minus_adjoint(left, right):
    return [
        [
            (left[i][j][0] - right[j][i][0], left[i][j][1] + right[j][i][1])
            for j in range(3)
        ]
        for i in range(3)
    ]


def mapped(function, matrix):
    return [[tuple(function(part) for part in item) for item in row] for row in matrix]


def rows_of(time):
    return pl.ds(pl.multiple_of(time * LX, LX), LX)


def next_time(time):
    return lax.rem(time + 1, LT)


def last_time(time):
    return lax.rem(time + LT - 1, LT)


def load_matrix(ref, direction, time, half=None):
    rows = rows_of(time) if not isinstance(time, int) else slice(time * LX, (time + 1) * LX)

    def load(part, i, j):
        value = ref[direction, part, i, j, rows, :].astype(F32)
        return value if half is None else value[half]

    return [[tuple(load(part, i, j) for part in (0, 1)) for j in range(3)] for i in range(3)]


def halved(matrix, half):
    return mapped(lambda value: value[half], matrix)


def up_x(value):
    return pltpu.roll(value, LX - 1, 0)


def down_x(value):
    return pltpu.roll(value, 1, 0)


def up_y(value):
    return pltpu.roll(value, LY - 1, 1)


def down_y(value):
    return pltpu.roll(value, 1, 1)


def neighbour_link(ref, direction, step, time):
    if step == 3:
        return load_matrix(ref, direction, next_time(time))
    return mapped(up_x if step == 0 else up_y, load_matrix(ref, direction, time))


def staple_kernel(links, *outs):
    def body(out, begin, step, carry):
        time = begin + step
        rows = rows_of(step)
        up_link = load_matrix(links, 2, time)
        for slot, direction in enumerate((0, 1, 3)):
            left = product(up_link, load_matrix(links, direction, time), left_dagger=True)
            staple = product(left, neighbour_link(links, 2, direction, time))
            for i in range(3):
                for j in range(3):
                    for part in (0, 1):
                        out[slot, part, i, j, rows, :] = staple[i][j][part].astype(BF16)
        return carry

    for out, (begin, end) in zip(outs, PIECES):
        lax.fori_loop(0, end - begin, functools.partial(body, out, jnp.int32(begin)), 0)


def flat_kernel(links, out, corner):
    def lower(time, carry):
        rows = rows_of(time)
        for slot, direction in enumerate((0, 1)):
            bent = product(
                load_matrix(links, direction, time), neighbour_link(links, 3, direction, time)
            )
            bent = product(load_matrix(links, 3, time), bent, left_dagger=True)
            for i in range(3):
                for j in range(3):
                    for part in (0, 1):
                        corner[slot, part, i, j, rows, :] = bent[i][j][part]
        return carry

    lax.fori_loop(0, LT, lower, 0)

    def upper(time, carry):
        rows = rows_of(time)
        for slot, direction in enumerate((0, 1)):
            far = product(
                load_matrix(links, 3, time), neighbour_link(links, direction, 3, time)
            )
            far = product(neighbour_link(links, 3, direction, time), far, right_dagger=True)
            bend = minus_adjoint(far, load_matrix(corner, slot, last_time(time)))
            link = load_matrix(links, direction, time)
            ahead = anti_product(link, bend)
            behind = anti_product(bend, link)
            move = down_x if direction == 0 else down_y
            for index in range(HALF):
                out[(slot + 1) * HALF + index, rows, :] = ahead[index] + move(behind[index])
        link_x, link_y = load_matrix(links, 0, time), load_matrix(links, 1, time)
        over_x, over_y = mapped(up_y, link_x), mapped(up_x, link_y)
        near = product(link_x, product(link_y, over_x), left_dagger=True)
        far = product(over_x, product(link_x, over_y), right_dagger=True)
        bend = minus_adjoint(far, mapped(down_x, near))
        ahead = anti_product(link_y, bend)
        behind = anti_product(bend, link_y)
        for index in range(HALF):
            out[index, rows, :] = -(ahead[index] + down_y(behind[index]))
        return carry

    lax.fori_loop(0, LT, upper, 0)


def neighbour_up(links, later, step):
    if step == 3:
        return load_matrix(later, 0, 0)
    return mapped(up_x if step == 0 else up_y, load_matrix(links, 2, 0))


def z_planes(links, later, above, staples, rise, edge):
    for half in HALVES:
        up_link = load_matrix(links, 2, 0, half)
        for slot, direction in enumerate((0, 1, 3)):
            far = product(up_link, load_matrix(above, slot, 0, half))
            moved = halved(neighbour_up(links, later, direction), half)
            far = product(moved, far, right_dagger=True)
            bend = minus_adjoint(far, load_matrix(staples, slot, 0, half))
            link = load_matrix(links, direction, 0, half)
            for index, value in enumerate(anti_product(link, bend)):
                rise[slot * HALF + index, half, :] = value
            for index, value in enumerate(anti_product(bend, link)):
                if direction == 1:
                    rise[HALF + index, half, :] += down_y(value)
                else:
                    edge[(0 if direction == 3 else HALF) + index, half, :] = value
    for index in range(HALF):
        rise[index] += down_x(edge[HALF + index])


def coefficients(flat, rise, before, coef):
    for block in range(2):
        sign = 1.0 if block == 0 else -1.0

        def field(number):
            parts = []
            for index in range(HALF):
                if number == 0:
                    value = sign * flat[HALF + index] - rise[HALF + index]
                elif number == 1:
                    value = -sign * flat[2 * HALF + index] - rise[index]
                else:
                    value = -flat[index] - sign * (rise[2 * HALF + index] + before[index])
                parts.append(value * 0.125)
            trace = (parts[3] + parts[4] + parts[5]) * (1.0 / 3.0)
            for index in (3, 4, 5):
                parts[index] = parts[index] - trace
            return parts

        first, second, third = field(0), field(1), field(2)
        for index in range(HALF):
            coef[block, index] = third[index] if index < 3 else -third[index]
        place = HALF
        for i in range(3):
            for j in range(3):
                if i == j:
                    re, im = -first[3 + i], second[3 + i]
                else:
                    index = UPPER.index((min(i, j), max(i, j)))
                    if i < j:
                        re = second[index] - first[6 + index]
                        im = first[index] + second[6 + index]
                    else:
                        re = -second[index] - first[6 + index]
                        im = second[6 + index] - first[index]
                coef[block, place] = re
                coef[block, place + 1] = im
                place += 2


def insert_slice(coef, plain, inserted, crossed):
    for block in range(2):
        for source in range(plain.shape[0]):
            rounded = {}
            for half in HALVES:
                spinor = [
                    [
                        tuple(
                            plain[source, part, 2 * block + spin, color].astype(F32)[half]
                            for part in (0, 1)
                        )
                        for color in range(3)
                    ]
                    for spin in range(2)
                ]
                for spin in range(2):
                    for i in range(3):
                        total_re = total_im = None
                        for j in range(3):
                            v_re, v_im = spinor[1 - spin][j]
                            row, column = (i, j) if spin == 0 else (j, i)
                            place = HALF + 2 * (3 * row + column)
                            m_re, m_im = coef[block, place, half, :], coef[block, place + 1, half, :]
                            re, im = m_re * v_re, m_re * v_im
                            total_re = re if total_re is None else total_re + re
                            total_im = im if total_im is None else total_im + im
                            if spin == 0:
                                total_re = total_re - m_im * v_im
                                total_im = total_im + m_im * v_re
                            else:
                                total_re = total_re + m_im * v_im
                                total_im = total_im - m_im * v_re
                        for j in range(3):
                            v_re, v_im = spinor[spin][j]
                            if i == j:
                                m_re, m_im = coef[block, 3 + i, half, :], None
                            else:
                                index = UPPER.index((min(i, j), max(i, j)))
                                m_re = coef[block, 6 + index, half, :]
                                m_im = coef[block, index, half, :]
                            if spin == 0:
                                total_re = total_re + m_re * v_re
                                total_im = total_im + m_re * v_im
                            else:
                                total_re = total_re - m_re * v_re
                                total_im = total_im - m_re * v_im
                            if m_im is not None:
                                if (i < j) == (spin == 0):
                                    total_re = total_re - m_im * v_im
                                    total_im = total_im + m_im * v_re
                                else:
                                    total_re = total_re + m_im * v_im
                                    total_im = total_im - m_im * v_re
                        for part, total in enumerate((total_re, total_im)):
                            rounded.setdefault((spin, i, part), []).append(total)
            for spin in range(2):
                result = []
                for i in range(3):
                    kept = []
                    for part in (0, 1):
                        value = jnp.concatenate(rounded[spin, i, part], axis=0).astype(BF16)
                        inserted[source, part, 2 * block + spin, i] = value
                        kept.append(value.astype(F32))
                    result.append(kept)
                vector = [
                    [plain[source, part, 2 * block + spin, color].astype(F32) for part in (0, 1)]
                    for color in range(3)
                ]
                for a, b, c in ((0, 1, 2), (1, 2, 0), (2, 0, 1)):
                    (a_re, a_im), (b_re, b_im) = result[a], result[b]
                    (p_re, p_im), (q_re, q_im) = vector[a], vector[b]
                    crossed[source, 0, 2 * block + spin, c] = (
                        a_re * q_re - a_im * q_im - b_re * p_re + b_im * p_im
                    )
                    crossed[source, 1, 2 * block + spin, c] = (
                        a_re * q_im + a_im * q_re - b_re * p_im - b_im * p_re
                    )


def insert_kernel(begin, end, *refs):
    first, last = begin == 0, end == LT
    refs = list(refs)
    links, later, above, staples, flat, plain = refs[:6]
    refs = refs[6:]
    if not first:
        edge_in = refs.pop(0)
        if last:
            rise_zero = refs.pop(0)
        refs = refs[2:]
    inserted, crossed = refs[:2]
    refs = refs[2:]
    edge_out = rise_out = None
    if not last:
        edge_out = refs.pop(0)
        if first:
            rise_out = refs.pop(0)
    rise, edge, coef = refs
    step = pl.program_id(0)
    steps = end - begin
    slot = jnp.minimum(lax.rem(step, steps), 1) if last and first else jnp.int32(0)
    turn = lax.rem(step, 2)

    if not first:

        @pl.when(step == 0)
        def _():
            edge[1, 0:HALF] = edge_in[...]

    @pl.when(step < steps)
    def _():
        z_planes(links, later, above, staples, rise.at[slot], edge.at[turn])

    if not last:

        @pl.when(step == steps - 1)
        def _():
            edge_out[...] = edge[turn, 0:HALF]

        if first:

            @pl.when(step == 0)
            def _():
                rise_out[...] = rise[0]

    if last and not first:

        @pl.when(step == steps)
        def _():
            rise[0] = rise_zero[...]

    @pl.when(step > 0 if first else step >= 0)
    def _():
        coefficients(flat, rise.at[slot], edge.at[1 - turn], coef)
        insert_slice(coef, plain, inserted, crossed)


def project_kernel(sources, crossed, sink, wave_y, wave_x, turn, owner, out, density):
    count = sources * LT * LX

    step = pl.program_id(0)
    for inner in range(sink.shape[0] // 2):
        rows = slice(inner * LX, (inner + 1) * LX)
        time = step * (sink.shape[0] // 2) + inner
        for source in range(sources):
            total_re = total_im = None
            for spin in range(4):
                for color in range(3):
                    eta = []
                    for part in (0, 1):
                        line = (((source * 2 + part) * 4) + spin) * 3 + color
                        lines = slice(line * 8, line * 8 + 8)
                        eta.append(
                            jnp.concatenate(
                                [sink[2 * inner + half, lines, :] for half in (0, 1)], axis=0
                            ).astype(F32)
                        )
                    w_re = crossed[source, 0, spin, color, rows, :]
                    w_im = crossed[source, 1, spin, color, rows, :]
                    re = w_re * eta[0] - w_im * eta[1]
                    im = w_re * eta[1] + w_im * eta[0]
                    total_re = re if total_re is None else total_re + re
                    total_im = im if total_im is None else total_im + im
            place = pl.multiple_of(source * TX + time * LX, LX)
            density[pl.ds(place, LX), :] = total_re
            density[pl.ds(pl.multiple_of(count + place, LX), LX), :] = total_im

    @pl.when(step == pl.num_programs(0) - 1)
    def _():
        project(sources, wave_y, wave_x, turn, owner, out, density)


def project(sources, wave_y, wave_x, turn, owner, out, density):
    count = sources * TX
    values = density[...]
    high = values.astype(BF16)
    low = (values - high.astype(F32)).astype(BF16)
    both = functools.partial(jnp.dot, preferred_element_type=F32)
    waves = both(high, wave_y[0]) + (both(low, wave_y[0]) + both(high, wave_y[1]))
    cos_re, sin_re = waves[:count, :NMOM], waves[:count, NMOM:]
    cos_im, sin_im = waves[count:, :NMOM], waves[count:, NMOM:]
    line_re = (cos_re + sin_im).reshape(sources * LT, LX, NMOM)
    line_im = (cos_im - sin_re).reshape(sources * LT, LX, NMOM)
    cos_x, sin_x = wave_x[0][None], wave_x[1][None]
    sum_re = jnp.sum(line_re * cos_x + line_im * sin_x, axis=1)
    sum_im = jnp.sum(line_im * cos_x - line_re * sin_x, axis=1)
    cos_t, sin_t = turn[0], turn[1]
    turned = jnp.concatenate(
        [sum_re * cos_t - sum_im * sin_t, sum_re * sin_t + sum_im * cos_t], axis=1
    )
    out[...] = jnp.dot(
        owner[...], turned, precision=lax.Precision.HIGHEST, preferred_element_type=F32
    )


def spread_kernel(sink, out):
    for device in range(out.shape[0]):
        piece = sink[:, :, device * LY : (device + 1) * LY].astype(F32)
        out[device] = piece.reshape(out.shape[1], LY).astype(BF16)


def params(megabytes=56):
    return pltpu.CompilerParams(vmem_limit_bytes=megabytes << 20)


def slab_block(lead, time_of):
    return pl.BlockSpec(
        tuple(lead) + (LX, LY), lambda step: (0,) * len(lead) + (time_of(step), 0)
    )


def up_block(time_of):
    return pl.BlockSpec((1, 2, 3, 3, LX, LY), lambda step: (2, 0, 0, 0, time_of(step), 0))


def whole(count):
    return [pl.BlockSpec(memory_space=pltpu.VMEM)] * count


def cost(flops, moved):
    return pl.CostEstimate(flops=flops, bytes_accessed=moved, transcendentals=0)


def momenta():
    index = np.arange(NMOM)
    return index % 4 - 1, index // 4 % 4 - 1, index // 16 - NMOM // 32


def wave_tables():
    wave_x, wave_y, _ = momenta()
    angle_y = 2.0 * np.pi * ((wave_y[None, :] * np.arange(LY)[:, None]) % LY) / LY
    table = np.concatenate([np.cos(angle_y), np.sin(angle_y)], axis=1)
    high = table.astype(jnp.bfloat16)
    low = (table - high.astype(np.float64)).astype(jnp.bfloat16)
    angle_x = 2.0 * np.pi * ((wave_x[None, :] * np.arange(LX)[:, None]) % LX) / LX
    along_x = np.stack([np.cos(angle_x), np.sin(angle_x)]).astype(np.float32)
    return np.stack([high, low]), along_x


def turn_table(source_place, z_position, extent_z):
    wave_x, wave_y, wave_z = (jnp.asarray(w, jnp.int32)[None, :] for w in momenta())
    fraction = (
        (wave_x * source_place[:, 0:1] % LX).astype(F32) / LX
        + (wave_y * source_place[:, 1:2] % LY).astype(F32) / LY
        + (wave_z * (source_place[:, 2:3] - z_position) % extent_z).astype(F32) / extent_z
    )
    angle = 2.0 * math.pi * fraction
    scale = OUTPUT_SCALE / math.sqrt(LX * LY * extent_z)
    table = jnp.stack([jnp.cos(angle), jnp.sin(angle)]) * scale
    return jnp.repeat(table, LT, axis=1)


def owner_table(source_time, pair_source, pair_separation, pair_owner, row_count):
    sources = source_time.shape[0]
    pairs = pair_source.shape[0]
    hits = pair_source[:, None] == jnp.arange(sources, dtype=jnp.int32)[None, :]
    start = jnp.sum(jnp.where(hits, source_time[None, :], 0), axis=1)
    chosen = pair_source * LT + (start + pair_separation) % LT
    picks = chosen[:, None] == jnp.arange(sources * LT, dtype=jnp.int32)[None, :]
    owner = pair_owner[:, 0]
    number = jnp.arange(pairs, dtype=jnp.int32)
    earlier = (owner[:, None] == owner[None, :]) & (number[None, :] < number[:, None])
    target = owner * PADDED + jnp.sum(earlier.astype(jnp.int32), axis=1)
    rows = jnp.arange(row_count, dtype=jnp.int32)[:, None] == target[None, :]
    return jnp.dot(rows.astype(BF16), picks.astype(BF16), preferred_element_type=F32)


def on_device(
    gauge_links,
    propagators,
    sink_cotangent,
    source_time,
    source_place,
    pair_source,
    pair_separation,
    pair_owner,
):
    devices = lax.axis_size("space")
    assert gauge_links.shape[5] == LY
    sources = propagators.shape[0]
    lines = sources * 2 * 4 * 3
    slab = TX // devices
    site = (TX, LY)

    matrices = (3, 2, 3, 3)
    own_staples = pl.pallas_call(
        staple_kernel,
        out_shape=[
            jax.ShapeDtypeStruct(matrices + ((end - begin) * LX, LY), BF16)
            for begin, end in PIECES
        ],
        in_specs=whole(1),
        out_specs=whole(len(PIECES)),
        compiler_params=params(16),
        cost_estimate=cost(1000, 1000),
        name="staples",
    )(gauge_links)
    above, staples = [], []
    for (begin, end), staple in zip(PIECES, own_staples):
        level = gauge_links[:, :, :, :, begin * LX : end * LX]
        level = jnp.concatenate([level[0:2], level[3:4]], axis=0)
        above.append(from_behind(level, -1))
        staples.append(from_behind(staple, 1))

    if slab == 8:
        spread = pl.pallas_call(
            spread_kernel,
            out_shape=jax.ShapeDtypeStruct((devices, lines * slab, LY), BF16),
            grid=(4,),
            in_specs=[pl.BlockSpec((lines, slab, devices // 4 * LY), lambda step: (0, 0, step))],
            out_specs=pl.BlockSpec((devices // 4, lines * slab, LY), lambda step: (step, 0, 0)),
            compiler_params=params(8),
            cost_estimate=cost(1000, 1000),
            name="spread",
        )(sink_cotangent.reshape(lines, slab, devices * LY))
    else:
        spread = (
            sink_cotangent.reshape(lines, slab, devices, LY)
            .transpose(2, 0, 1, 3)
            .reshape(devices, lines * slab, LY)
        )
    sink = lax.all_to_all(spread, "space", split_axis=0, concat_axis=0, tiled=True)
    if slab != 8:
        sink = (
            sink.reshape(TX // 8, 8 // slab, lines, slab, LY)
            .transpose(0, 2, 1, 3, 4)
            .reshape(TX // 8, lines * 8, LY)
        )

    flat = pl.pallas_call(
        flat_kernel,
        out_shape=jax.ShapeDtypeStruct((3 * HALF,) + site, F32),
        in_specs=whole(1),
        out_specs=whole(1)[0],
        scratch_shapes=[pltpu.VMEM((2, 2, 3, 3) + site, F32)],
        compiler_params=params(16),
        cost_estimate=cost(1000, 1000),
        name="flat_planes",
    )(gauge_links)

    spinors = propagators.shape[:4]

    inserted = crossed = edge = rise_zero = None
    for index, (begin, end) in enumerate(PIECES):
        first, last = begin == 0, end == LT

        def now(step):
            return lax.rem(begin + step, LT)

        def own(step):
            return jnp.minimum(step, end - begin - 1)

        def later(step):
            return lax.rem(begin + step + 1, LT)

        def written(step):
            return lax.rem(begin + (jnp.maximum(step, 1) if first else step), LT)

        operands = [gauge_links, gauge_links, above[index], staples[index], flat, propagators]
        specs = [
            slab_block((4, 2, 3, 3), now),
            up_block(later),
            slab_block(matrices, own),
            slab_block(matrices, own),
            slab_block((3 * HALF,), now),
            slab_block(spinors, now),
        ]
        shapes = [
            jax.ShapeDtypeStruct(propagators.shape, BF16),
            jax.ShapeDtypeStruct(propagators.shape, F32),
        ]
        out_specs = [slab_block(spinors, written), slab_block(spinors, written)]
        aliases = {}
        if not first:
            operands.append(edge)
            specs += whole(1)
            if last:
                operands.append(rise_zero)
                specs += whole(1)
            aliases = {len(operands): 0, len(operands) + 1: 1}
            operands += [inserted, crossed]
            specs += [pl.BlockSpec(memory_space=pl.ANY)] * 2
        if not last:
            shapes.append(jax.ShapeDtypeStruct((HALF, LX, LY), F32))
            out_specs += whole(1)
            if first:
                shapes.append(jax.ShapeDtypeStruct((3 * HALF, LX, LY), F32))
                out_specs += whole(1)
        results = pl.pallas_call(
            functools.partial(insert_kernel, begin, end),
            grid=(end - begin + last,),
            out_shape=shapes,
            in_specs=specs,
            out_specs=out_specs,
            input_output_aliases=aliases,
            scratch_shapes=[
                pltpu.VMEM((2, 3 * HALF, LX, LY), F32),
                pltpu.VMEM((2, 2 * HALF, LX, LY), F32),
                pltpu.VMEM((2, HALF + 18, LX, LY), F32),
            ],
            compiler_params=params(),
            cost_estimate=cost(10**12, 1000),
            name="insertion",
        )(*operands)
        inserted, crossed = results[:2]
        if not last:
            edge = results[2]
            if first:
                rise_zero = results[3]

    table_y, table_x = wave_tables()
    turn = turn_table(source_place, lax.axis_index("space"), devices)
    owner = owner_table(
        source_time, pair_source, pair_separation, pair_owner, devices * PADDED
    )
    steps = 4
    rows = pl.pallas_call(
        functools.partial(project_kernel, sources),
        grid=(steps,),
        out_shape=jax.ShapeDtypeStruct((devices * PADDED, 2 * NMOM), F32),
        in_specs=[
            pl.BlockSpec(spinors + (TX // steps, LY), lambda step: (0, 0, 0, 0, step, 0)),
            pl.BlockSpec((TX // 8 // steps, lines * 8, LY), lambda step: (step, 0, 0)),
        ]
        + whole(4),
        out_specs=whole(1)[0],
        scratch_shapes=[pltpu.VMEM((2 * sources * TX, LY), F32)],
        compiler_params=params(),
        cost_estimate=cost(1000, 1000),
        name="projection",
    )(crossed, sink, jnp.asarray(table_y), jnp.asarray(table_x), turn, owner)
    parts = lax.all_to_all(
        rows.reshape(devices, PADDED, 2 * NMOM), "space", split_axis=0, concat_axis=0, tiled=True
    )
    return inserted, jnp.sum(parts[:, :SLOTS], axis=0)


def solution(mesh):
    placed = (
        P("grp", None, None, None, None, "space"),
        P("grp", None, None, None, None, "space"),
        P("grp", None, None, None, "space", None),
        P("grp"),
        P("grp", None),
        P("grp"),
        P("grp"),
        P("grp", None),
    )
    return jax.shard_map(
        on_device,
        mesh=mesh,
        in_specs=placed,
        out_specs=(P("grp", None, None, None, None, "space"), P(("grp", "space"), None)),
        check_vma=False,
    )
```

```python
import functools
import math

import jax
import jax.numpy as jnp
import numpy as np
from jax import lax
from jax.experimental import pallas as pl
from jax.experimental.pallas import tpu as pltpu
from jax.sharding import PartitionSpec as P

LT = 8
LX = 16
LY = 128
TX = LT * LX
NMOM = 128
SLOTS = 4
OUTPUT_SCALE = 0.1
F32 = jnp.float32
BF16 = jnp.bfloat16
PIECES = ((0, 5), (5, 8))
PADDED = 8
UPPER = ((0, 1), (0, 2), (1, 2))
SYMMETRIC = ((0, 0), (1, 1), (2, 2), (0, 1), (0, 2), (1, 2))
HALVES = (slice(0, 8), slice(8, 16))
HALF = len(UPPER) + len(SYMMETRIC)


def from_behind(block, distance):
    count = lax.axis_size("space")
    return lax.ppermute(block, "space", [((i - distance) % count, i) for i in range(count)])


def entry(left, right, row, col, left_dagger, right_dagger, part):
    total = None
    for inner in range(3):
        a_re, a_im = left[inner][row] if left_dagger else left[row][inner]
        b_re, b_im = right[col][inner] if right_dagger else right[inner][col]
        if part == 0:
            first, second = a_re * b_re, a_im * b_im
            negative = left_dagger == right_dagger
        elif left_dagger:
            first, second = a_re * b_im, a_im * b_re
            negative = True
        else:
            first, second = a_im * b_re, a_re * b_im
            negative = right_dagger
        total = first if total is None else total + first
        total = total - second if negative else total + second
    return total


def product(left, right, left_dagger=False, right_dagger=False):
    return [
        [
            tuple(entry(left, right, i, j, left_dagger, right_dagger, part) for part in (0, 1))
            for j in range(3)
        ]
        for i in range(3)
    ]


def anti_product(left, right):
    kept = []
    for i, j in UPPER:
        kept.append(entry(left, right, i, j, False, False, 0) - entry(left, right, j, i, False, False, 0))
    for i, j in SYMMETRIC:
        value = entry(left, right, i, j, False, False, 1)
        kept.append(value + (value if i == j else entry(left, right, j, i, False, False, 1)))
    return kept


def minus_adjoint(left, right):
    return [
        [
            (left[i][j][0] - right[j][i][0], left[i][j][1] + right[j][i][1])
            for j in range(3)
        ]
        for i in range(3)
    ]


def mapped(function, matrix):
    return [[tuple(function(part) for part in item) for item in row] for row in matrix]


def rows_of(time):
    return pl.ds(pl.multiple_of(time * LX, LX), LX)


def next_time(time):
    return lax.rem(time + 1, LT)


def last_time(time):
    return lax.rem(time + LT - 1, LT)


def load_matrix(ref, direction, time, half=None):
    rows = rows_of(time) if not isinstance(time, int) else slice(time * LX, (time + 1) * LX)

    def load(part, i, j):
        value = ref[direction, part, i, j, rows, :].astype(F32)
        return value if half is None else value[half]

    return [[tuple(load(part, i, j) for part in (0, 1)) for j in range(3)] for i in range(3)]


def load_line(ref, slot, half):
    def load(part, i, j):
        return ref[0, ((slot * 2 + part) * 3 + i) * 3 + j].astype(F32)[half]

    return [[tuple(load(part, i, j) for part in (0, 1)) for j in range(3)] for i in range(3)]


def halved(matrix, half):
    return mapped(lambda value: value[half], matrix)


def up_x(value):
    return pltpu.roll(value, LX - 1, 0)


def down_x(value):
    return pltpu.roll(value, 1, 0)


def up_y(value):
    return pltpu.roll(value, LY - 1, 1)


def down_y(value):
    return pltpu.roll(value, 1, 1)


def neighbour_link(ref, direction, step, time):
    if step == 3:
        return load_matrix(ref, direction, next_time(time))
    return mapped(up_x if step == 0 else up_y, load_matrix(ref, direction, time))


def staple_kernel(begin, level, upward, out):
    def body(step, carry):
        time = begin + step
        up_link = load_matrix(upward, 0, time)
        for slot in range(3):
            left = product(up_link, load_matrix(level, slot, step), left_dagger=True)
            direction = (0, 1, 3)[slot]
            staple = product(left, neighbour_link(upward, 0, direction, time))
            for i in range(3):
                for j in range(3):
                    for part in (0, 1):
                        out[step, ((slot * 2 + part) * 3 + i) * 3 + j] = staple[i][j][part].astype(BF16)
        return carry

    lax.fori_loop(0, out.shape[0], body, 0)


def flat_kernel(links, out, corner):
    def lower(time, carry):
        rows = rows_of(time)
        for slot, direction in enumerate((0, 1)):
            bent = product(
                load_matrix(links, direction, time), neighbour_link(links, 3, direction, time)
            )
            bent = product(load_matrix(links, 3, time), bent, left_dagger=True)
            for i in range(3):
                for j in range(3):
                    for part in (0, 1):
                        corner[slot, part, i, j, rows, :] = bent[i][j][part]
        return carry

    lax.fori_loop(0, LT, lower, 0)

    def upper(time, carry):
        for slot, direction in enumerate((0, 1)):
            far = product(
                load_matrix(links, 3, time), neighbour_link(links, direction, 3, time)
            )
            far = product(neighbour_link(links, 3, direction, time), far, right_dagger=True)
            bend = minus_adjoint(far, load_matrix(corner, slot, last_time(time)))
            link = load_matrix(links, direction, time)
            ahead = anti_product(link, bend)
            behind = anti_product(bend, link)
            move = down_x if direction == 0 else down_y
            for index in range(HALF):
                out[time, (slot + 1) * HALF + index] = ahead[index] + move(behind[index])
        link_x, link_y = load_matrix(links, 0, time), load_matrix(links, 1, time)
        over_x, over_y = mapped(up_y, link_x), mapped(up_x, link_y)
        near = product(link_x, product(link_y, over_x), left_dagger=True)
        far = product(over_x, product(link_x, over_y), right_dagger=True)
        bend = minus_adjoint(far, mapped(down_x, near))
        ahead = anti_product(link_y, bend)
        behind = anti_product(bend, link_y)
        for index in range(HALF):
            out[time, index] = -(ahead[index] + down_y(behind[index]))
        return carry

    lax.fori_loop(0, LT, upper, 0)


def neighbour_up(links, later, step):
    if step == 3:
        return load_matrix(later, 0, 0)
    return mapped(up_x if step == 0 else up_y, load_matrix(links, 2, 0))


def z_planes(links, later, above, staples, rise, edge):
    for half in HALVES:
        up_link = load_matrix(links, 2, 0, half)
        for slot, direction in enumerate((0, 1, 3)):
            far = product(up_link, load_matrix(above, slot, 0, half))
            moved = halved(neighbour_up(links, later, direction), half)
            far = product(moved, far, right_dagger=True)
            bend = minus_adjoint(far, load_line(staples, slot, half))
            link = load_matrix(links, direction, 0, half)
            for index, value in enumerate(anti_product(link, bend)):
                rise[slot * HALF + index, half, :] = value
            for index, value in enumerate(anti_product(bend, link)):
                if direction == 1:
                    rise[HALF + index, half, :] += down_y(value)
                else:
                    edge[(0 if direction == 3 else HALF) + index, half, :] = value
    for index in range(HALF):
        rise[index] += down_x(edge[HALF + index])


def coefficients(flat, rise, before, coef):
    for block in range(2):
        sign = 1.0 if block == 0 else -1.0

        def field(number):
            parts = []
            for index in range(HALF):
                if number == 0:
                    value = sign * flat[HALF + index] - rise[HALF + index]
                elif number == 1:
                    value = -sign * flat[2 * HALF + index] - rise[index]
                else:
                    value = -flat[index] - sign * (rise[2 * HALF + index] + before[index])
                parts.append(value * 0.125)
            trace = (parts[3] + parts[4] + parts[5]) * (1.0 / 3.0)
            for index in (3, 4, 5):
                parts[index] = parts[index] - trace
            return parts

        first, second, third = field(0), field(1), field(2)
        for index in range(HALF):
            coef[block, index] = third[index] if index < 3 else -third[index]
        place = HALF
        for i in range(3):
            for j in range(3):
                if i == j:
                    re, im = -first[3 + i], second[3 + i]
                else:
                    index = UPPER.index((min(i, j), max(i, j)))
                    if i < j:
                        re = second[index] - first[6 + index]
                        im = first[index] + second[6 + index]
                    else:
                        re = -second[index] - first[6 + index]
                        im = second[6 + index] - first[index]
                coef[block, place] = re
                coef[block, place + 1] = im
                place += 2


def insert_slice(coef, plain, inserted, crossed):
    for block in range(2):
        for source in range(plain.shape[0]):
            rounded = {}
            for half in HALVES:
                spinor = [
                    [
                        tuple(
                            plain[source, part, 2 * block + spin, color].astype(F32)[half]
                            for part in (0, 1)
                        )
                        for color in range(3)
                    ]
                    for spin in range(2)
                ]
                for spin in range(2):
                    for i in range(3):
                        total_re = total_im = None
                        for j in range(3):
                            v_re, v_im = spinor[1 - spin][j]
                            row, column = (i, j) if spin == 0 else (j, i)
                            place = HALF + 2 * (3 * row + column)
                            m_re, m_im = coef[block, place, half, :], coef[block, place + 1, half, :]
                            re, im = m_re * v_re, m_re * v_im
                            total_re = re if total_re is None else total_re + re
                            total_im = im if total_im is None else total_im + im
                            if spin == 0:
                                total_re = total_re - m_im * v_im
                                total_im = total_im + m_im * v_re
                            else:
                                total_re = total_re + m_im * v_im
                                total_im = total_im - m_im * v_re
                        for j in range(3):
                            v_re, v_im = spinor[spin][j]
                            if i == j:
                                m_re, m_im = coef[block, 3 + i, half, :], None
                            else:
                                index = UPPER.index((min(i, j), max(i, j)))
                                m_re = coef[block, 6 + index, half, :]
                                m_im = coef[block, index, half, :]
                            if spin == 0:
                                total_re = total_re + m_re * v_re
                                total_im = total_im + m_re * v_im
                            else:
                                total_re = total_re - m_re * v_re
                                total_im = total_im - m_re * v_im
                            if m_im is not None:
                                if (i < j) == (spin == 0):
                                    total_re = total_re - m_im * v_im
                                    total_im = total_im + m_im * v_re
                                else:
                                    total_re = total_re + m_im * v_im
                                    total_im = total_im - m_im * v_re
                        for part, total in enumerate((total_re, total_im)):
                            rounded.setdefault((spin, i, part), []).append(total)
            for spin in range(2):
                result = []
                for i in range(3):
                    kept = []
                    for part in (0, 1):
                        value = jnp.concatenate(rounded[spin, i, part], axis=0).astype(BF16)
                        inserted[source, part, 2 * block + spin, i] = value
                        kept.append(value.astype(F32))
                    result.append(kept)
                vector = [
                    [plain[source, part, 2 * block + spin, color].astype(F32) for part in (0, 1)]
                    for color in range(3)
                ]
                for a, b, c in ((0, 1, 2), (1, 2, 0), (2, 0, 1)):
                    (a_re, a_im), (b_re, b_im) = result[a], result[b]
                    (p_re, p_im), (q_re, q_im) = vector[a], vector[b]
                    crossed[0, ((source * 2) * 4 + 2 * block + spin) * 3 + c] = (
                        a_re * q_re - a_im * q_im - b_re * p_re + b_im * p_im
                    )
                    crossed[0, ((source * 2 + 1) * 4 + 2 * block + spin) * 3 + c] = (
                        a_re * q_im + a_im * q_re - b_re * p_im - b_im * p_re
                    )


def insert_kernel(begin, end, *refs):
    first, last = begin == 0, end == LT
    refs = list(refs)
    links, later, above, staples, flat, plain = refs[:6]
    refs = refs[6:]
    if not first:
        edge_in = refs.pop(0)
        if last:
            rise_zero = refs.pop(0)
        refs = refs[2:]
    inserted, crossed = refs[:2]
    refs = refs[2:]
    edge_out = rise_out = None
    if not last:
        edge_out = refs.pop(0)
        if first:
            rise_out = refs.pop(0)
    rise, edge, coef = refs
    step = pl.program_id(0)
    steps = end - begin
    slot = jnp.minimum(lax.rem(step, steps), 1) if last and first else jnp.int32(0)
    turn = lax.rem(step, 2)

    if not first:

        @pl.when(step == 0)
        def _():
            edge[1, 0:HALF] = edge_in[...]

    @pl.when(step < steps)
    def _():
        z_planes(links, later, above, staples, rise.at[slot], edge.at[turn])

    if not last:

        @pl.when(step == steps - 1)
        def _():
            edge_out[...] = edge[turn, 0:HALF]

        if first:

            @pl.when(step == 0)
            def _():
                rise_out[...] = rise[0]

    if last and not first:

        @pl.when(step == steps)
        def _():
            rise[0] = rise_zero[...]

    @pl.when(step > 0 if first else step >= 0)
    def _():
        coefficients(flat.at[0], rise.at[slot], edge.at[1 - turn], coef)
        insert_slice(coef, plain, inserted, crossed)


def project_kernel(sources, crossed, sink, wave_y, wave_x, turn, owner, out, density):
    count = sources * LT * LX

    step = pl.program_id(0)
    for inner in range(sink.shape[0] // 2):
        time = step * (sink.shape[0] // 2) + inner
        for source in range(sources):
            total_re = total_im = None
            for spin in range(4):
                for color in range(3):
                    eta = []
                    for part in (0, 1):
                        line = (((source * 2 + part) * 4) + spin) * 3 + color
                        lines = slice(line * 8, line * 8 + 8)
                        eta.append(
                            jnp.concatenate(
                                [sink[2 * inner + half, lines, :].astype(F32) for half in (0, 1)],
                                axis=0,
                            )
                        )
                    w_re = crossed[inner, ((source * 2) * 4 + spin) * 3 + color]
                    w_im = crossed[inner, ((source * 2 + 1) * 4 + spin) * 3 + color]
                    re = w_re * eta[0] - w_im * eta[1]
                    im = w_re * eta[1] + w_im * eta[0]
                    total_re = re if total_re is None else total_re + re
                    total_im = im if total_im is None else total_im + im
            place = pl.multiple_of(source * TX + time * LX, LX)
            density[pl.ds(place, LX), :] = total_re
            density[pl.ds(pl.multiple_of(count + place, LX), LX), :] = total_im

    @pl.when(step == pl.num_programs(0) - 1)
    def _():
        project(sources, wave_y, wave_x, turn, owner, out, density)


def project(sources, wave_y, wave_x, turn, owner, out, density):
    count = sources * TX
    values = density[...]
    high = values.astype(BF16)
    low = (values - high.astype(F32)).astype(BF16)
    both = functools.partial(jnp.dot, preferred_element_type=F32)
    waves = both(high, wave_y[0]) + (both(low, wave_y[0]) + both(high, wave_y[1]))
    cos_re, sin_re = waves[:count, :NMOM], waves[:count, NMOM:]
    cos_im, sin_im = waves[count:, :NMOM], waves[count:, NMOM:]
    line_re = (cos_re + sin_im).reshape(sources * LT, LX, NMOM)
    line_im = (cos_im - sin_re).reshape(sources * LT, LX, NMOM)
    cos_x, sin_x = wave_x[0][None], wave_x[1][None]
    sum_re = jnp.sum(line_re * cos_x + line_im * sin_x, axis=1)
    sum_im = jnp.sum(line_im * cos_x - line_re * sin_x, axis=1)
    cos_t, sin_t = turn[0], turn[1]
    turned = jnp.concatenate(
        [sum_re * cos_t - sum_im * sin_t, sum_re * sin_t + sum_im * cos_t], axis=1
    )
    out[...] = jnp.dot(
        owner[...], turned, precision=lax.Precision.HIGHEST, preferred_element_type=F32
    )


def pack_kernel(links, *refs):
    outs, upward, sems = refs[: len(PIECES)], refs[len(PIECES)], refs[-1]
    copies = []
    for index, (out, (begin, end)) in enumerate(zip(outs, PIECES)):
        rows = slice(begin * LX, end * LX)
        for part, (place, source) in enumerate(((slice(0, 2), slice(0, 2)), (slice(2, 3), slice(3, 4)))):
            copies.append(
                pltpu.make_async_copy(
                    links.at[source, :, :, :, rows], out.at[place], sems.at[2 * index + part]
                )
            )
    copies.append(pltpu.make_async_copy(links.at[2:3], upward, sems.at[2 * len(PIECES)]))
    for copy in copies:
        copy.start()
    for copy in copies:
        copy.wait()


def spread_kernel(sink, out):
    for device in range(out.shape[0]):
        piece = sink[:, :, device * LY : (device + 1) * LY].astype(F32)
        out[device] = piece.reshape(out.shape[1], LY).astype(BF16)


def params(megabytes=56):
    return pltpu.CompilerParams(vmem_limit_bytes=megabytes << 20)


def slab_block(lead, time_of):
    return pl.BlockSpec(
        tuple(lead) + (LX, LY), lambda step: (0,) * len(lead) + (time_of(step), 0)
    )


def up_block(time_of):
    return pl.BlockSpec((1, 2, 3, 3, LX, LY), lambda step: (2, 0, 0, 0, time_of(step), 0))


def whole(count):
    return [pl.BlockSpec(memory_space=pltpu.VMEM)] * count


def cost(flops, moved):
    return pl.CostEstimate(flops=flops, bytes_accessed=moved, transcendentals=0)


def momenta():
    index = np.arange(NMOM)
    return index % 4 - 1, index // 4 % 4 - 1, index // 16 - NMOM // 32


def wave_tables():
    wave_x, wave_y, _ = momenta()
    angle_y = 2.0 * np.pi * ((wave_y[None, :] * np.arange(LY)[:, None]) % LY) / LY
    table = np.concatenate([np.cos(angle_y), np.sin(angle_y)], axis=1)
    high = table.astype(jnp.bfloat16)
    low = (table - high.astype(np.float64)).astype(jnp.bfloat16)
    angle_x = 2.0 * np.pi * ((wave_x[None, :] * np.arange(LX)[:, None]) % LX) / LX
    along_x = np.stack([np.cos(angle_x), np.sin(angle_x)]).astype(np.float32)
    return np.stack([high, low]), along_x


def turn_table(source_place, z_position, extent_z):
    wave_x, wave_y, wave_z = (jnp.asarray(w, jnp.int32)[None, :] for w in momenta())
    fraction = (
        (wave_x * source_place[:, 0:1] % LX).astype(F32) / LX
        + (wave_y * source_place[:, 1:2] % LY).astype(F32) / LY
        + (wave_z * (source_place[:, 2:3] - z_position) % extent_z).astype(F32) / extent_z
    )
    angle = 2.0 * math.pi * fraction
    scale = OUTPUT_SCALE / math.sqrt(LX * LY * extent_z)
    table = jnp.stack([jnp.cos(angle), jnp.sin(angle)]) * scale
    return jnp.repeat(table, LT, axis=1)


def owner_table(source_time, pair_source, pair_separation, pair_owner, row_count):
    sources = source_time.shape[0]
    pairs = pair_source.shape[0]
    hits = pair_source[:, None] == jnp.arange(sources, dtype=jnp.int32)[None, :]
    start = jnp.sum(jnp.where(hits, source_time[None, :], 0), axis=1)
    chosen = pair_source * LT + (start + pair_separation) % LT
    picks = chosen[:, None] == jnp.arange(sources * LT, dtype=jnp.int32)[None, :]
    owner = pair_owner[:, 0]
    number = jnp.arange(pairs, dtype=jnp.int32)
    earlier = (owner[:, None] == owner[None, :]) & (number[None, :] < number[:, None])
    target = owner * PADDED + jnp.sum(earlier.astype(jnp.int32), axis=1)
    rows = jnp.arange(row_count, dtype=jnp.int32)[:, None] == target[None, :]
    return jnp.dot(rows.astype(BF16), picks.astype(BF16), preferred_element_type=F32)


def on_device(
    gauge_links,
    propagators,
    sink_cotangent,
    source_time,
    source_place,
    pair_source,
    pair_separation,
    pair_owner,
):
    devices = lax.axis_size("space")
    assert gauge_links.shape[5] == LY
    sources = propagators.shape[0]
    lines = sources * 2 * 4 * 3
    slab = TX // devices
    site = (TX, LY)

    matrices = (3, 2, 3, 3)
    *levels, upward = pl.pallas_call(
        pack_kernel,
        out_shape=[
            jax.ShapeDtypeStruct(matrices + ((end - begin) * LX, LY), BF16)
            for begin, end in PIECES
        ]
        + [jax.ShapeDtypeStruct((1, 2, 3, 3) + site, BF16)],
        in_specs=[pl.BlockSpec(memory_space=pl.ANY)],
        out_specs=whole(len(PIECES) + 1),
        scratch_shapes=[pltpu.SemaphoreType.DMA((2 * len(PIECES) + 1,))],
        compiler_params=params(6),
        cost_estimate=cost(1000, 1000),
        name="pack",
    )(gauge_links)
    def piece_staples(index):
        begin, end = PIECES[index]
        return pl.pallas_call(
            functools.partial(staple_kernel, begin),
            out_shape=jax.ShapeDtypeStruct((end - begin, 54, LX, LY), BF16),
            in_specs=whole(2),
            out_specs=whole(1)[0],
            compiler_params=params(12),
            cost_estimate=cost(1000, 1000),
            name="staples",
        )(levels[index], upward)

    above = [from_behind(level, -1) for level in levels]
    staples = [from_behind(piece_staples(0), 1)]

    if slab == 8:
        spread = pl.pallas_call(
            spread_kernel,
            out_shape=jax.ShapeDtypeStruct((devices, lines * slab, LY), BF16),
            grid=(4,),
            in_specs=[pl.BlockSpec((lines, slab, devices // 4 * LY), lambda step: (0, 0, step))],
            out_specs=pl.BlockSpec((devices // 4, lines * slab, LY), lambda step: (step, 0, 0)),
            compiler_params=params(8),
            cost_estimate=cost(1000, 1000),
            name="spread",
        )(sink_cotangent.reshape(lines, slab, devices * LY))
    else:
        spread = (
            sink_cotangent.reshape(lines, slab, devices, LY)
            .transpose(2, 0, 1, 3)
            .reshape(devices, lines * slab, LY)
        )
    sink = lax.all_to_all(spread, "space", split_axis=0, concat_axis=0, tiled=True)
    if slab != 8:
        sink = (
            sink.reshape(TX // 8, 8 // slab, lines, slab, LY)
            .transpose(0, 2, 1, 3, 4)
            .reshape(TX // 8, lines * 8, LY)
        )

    staples += [from_behind(piece_staples(index), 1) for index in range(1, len(PIECES))]

    flat = pl.pallas_call(
        flat_kernel,
        out_shape=jax.ShapeDtypeStruct((LT, 3 * HALF, LX, LY), F32),
        in_specs=whole(1),
        out_specs=whole(1)[0],
        scratch_shapes=[pltpu.VMEM((2, 2, 3, 3) + site, F32)],
        compiler_params=params(),
        cost_estimate=cost(1000, 1000),
        name="flat_planes",
    )(gauge_links)

    spinors = propagators.shape[:4]

    inserted = crossed = edge = rise_zero = None
    for index, (begin, end) in enumerate(PIECES):
        first, last = begin == 0, end == LT

        def now(step):
            return lax.rem(begin + step, LT)

        def own(step):
            return jnp.minimum(step, end - begin - 1)

        def later(step):
            return lax.rem(begin + step + 1, LT)

        def written(step):
            return lax.rem(begin + (jnp.maximum(step, 1) if first else step), LT)

        operands = [gauge_links, gauge_links, above[index], staples[index], flat, propagators]
        specs = [
            slab_block((4, 2, 3, 3), now),
            up_block(later),
            slab_block(matrices, own),
            pl.BlockSpec((1, 54, LX, LY), lambda step: (own(step), 0, 0, 0)),
            pl.BlockSpec((1, 3 * HALF, LX, LY), lambda step: (now(step), 0, 0, 0)),
            slab_block(spinors, now),
        ]
        shapes = [
            jax.ShapeDtypeStruct(propagators.shape, BF16),
            jax.ShapeDtypeStruct((LT, lines, LX, LY), F32),
        ]
        out_specs = [
            slab_block(spinors, written),
            pl.BlockSpec((1, lines, LX, LY), lambda step: (written(step), 0, 0, 0)),
        ]
        aliases = {}
        if not first:
            operands.append(edge)
            specs += whole(1)
            if last:
                operands.append(rise_zero)
                specs += whole(1)
            aliases = {len(operands): 0, len(operands) + 1: 1}
            operands += [inserted, crossed]
            specs += [pl.BlockSpec(memory_space=pl.ANY)] * 2
        if not last:
            shapes.append(jax.ShapeDtypeStruct((HALF, LX, LY), F32))
            out_specs += whole(1)
            if first:
                shapes.append(jax.ShapeDtypeStruct((3 * HALF, LX, LY), F32))
                out_specs += whole(1)
        results = pl.pallas_call(
            functools.partial(insert_kernel, begin, end),
            grid=(end - begin + last,),
            out_shape=shapes,
            in_specs=specs,
            out_specs=out_specs,
            input_output_aliases=aliases,
            scratch_shapes=[
                pltpu.VMEM((2, 3 * HALF, LX, LY), F32),
                pltpu.VMEM((2, 2 * HALF, LX, LY), F32),
                pltpu.VMEM((2, HALF + 18, LX, LY), F32),
            ],
            compiler_params=params(),
            cost_estimate=cost(10**12, 1000),
            name="insertion",
        )(*operands)
        inserted, crossed = results[:2]
        if not last:
            edge = results[2]
            if first:
                rise_zero = results[3]

    table_y, table_x = wave_tables()
    turn = turn_table(source_place, lax.axis_index("space"), devices)
    owner = owner_table(
        source_time, pair_source, pair_separation, pair_owner, devices * PADDED
    )
    steps = 2
    rows = pl.pallas_call(
        functools.partial(project_kernel, sources),
        grid=(steps,),
        out_shape=jax.ShapeDtypeStruct((devices * PADDED, 2 * NMOM), F32),
        in_specs=[
            pl.BlockSpec((LT // steps, lines, LX, LY), lambda step: (step, 0, 0, 0)),
            pl.BlockSpec((TX // 8 // steps, lines * 8, LY), lambda step: (step, 0, 0)),
        ]
        + whole(4),
        out_specs=whole(1)[0],
        scratch_shapes=[pltpu.VMEM((2 * sources * TX, LY), F32)],
        compiler_params=params(),
        cost_estimate=cost(1000, 1000),
        name="projection",
    )(crossed, sink, jnp.asarray(table_y), jnp.asarray(table_x), turn, owner)
    parts = lax.all_to_all(
        rows.reshape(devices, PADDED, 2 * NMOM), "space", split_axis=0, concat_axis=0, tiled=True
    )
    return inserted, jnp.sum(parts[:, :SLOTS], axis=0)


def solution(mesh):
    placed = (
        P("grp", None, None, None, None, "space"),
        P("grp", None, None, None, None, "space"),
        P("grp", None, None, None, "space", None),
        P("grp"),
        P("grp", None),
        P("grp"),
        P("grp"),
        P("grp", None),
    )
    return jax.shard_map(
        on_device,
        mesh=mesh,
        in_specs=placed,
        out_specs=(P("grp", None, None, None, None, "space"), P(("grp", "space"), None)),
        check_vma=False,
    )
```

```python
import functools
import math

import jax
import jax.numpy as jnp
import numpy as np
from jax import lax
from jax.experimental import pallas as pl
from jax.experimental.pallas import tpu as pltpu
from jax.sharding import PartitionSpec as P

LT = 8
LX = 16
LY = 128
TX = LT * LX
NMOM = 128
SLOTS = 4
OUTPUT_SCALE = 0.1
F32 = jnp.float32
BF16 = jnp.bfloat16
PIECES = ((0, 5), (5, 8))
PADDED = 8
UPPER = ((0, 1), (0, 2), (1, 2))
SYMMETRIC = ((0, 0), (1, 1), (2, 2), (0, 1), (0, 2), (1, 2))
HALVES = (slice(0, 8), slice(8, 16))
HALF = len(UPPER) + len(SYMMETRIC)


def from_behind(block, distance):
    count = lax.axis_size("space")
    return lax.ppermute(block, "space", [((i - distance) % count, i) for i in range(count)])


def entry(left, right, row, col, left_dagger, right_dagger, part):
    total = None
    for inner in range(3):
        a_re, a_im = left[inner][row] if left_dagger else left[row][inner]
        b_re, b_im = right[col][inner] if right_dagger else right[inner][col]
        if part == 0:
            first, second = a_re * b_re, a_im * b_im
            negative = left_dagger == right_dagger
        elif left_dagger:
            first, second = a_re * b_im, a_im * b_re
            negative = True
        else:
            first, second = a_im * b_re, a_re * b_im
            negative = right_dagger
        total = first if total is None else total + first
        total = total - second if negative else total + second
    return total


def product(left, right, left_dagger=False, right_dagger=False):
    return [
        [
            tuple(entry(left, right, i, j, left_dagger, right_dagger, part) for part in (0, 1))
            for j in range(3)
        ]
        for i in range(3)
    ]


def anti_product(left, right):
    kept = []
    for i, j in UPPER:
        kept.append(entry(left, right, i, j, False, False, 0) - entry(left, right, j, i, False, False, 0))
    for i, j in SYMMETRIC:
        value = entry(left, right, i, j, False, False, 1)
        kept.append(value + (value if i == j else entry(left, right, j, i, False, False, 1)))
    return kept


def minus_adjoint(left, right):
    return [
        [
            (left[i][j][0] - right[j][i][0], left[i][j][1] + right[j][i][1])
            for j in range(3)
        ]
        for i in range(3)
    ]


def mapped(function, matrix):
    return [[tuple(function(part) for part in item) for item in row] for row in matrix]


def rows_of(time):
    return pl.ds(pl.multiple_of(time * LX, LX), LX)


def next_time(time):
    return lax.rem(time + 1, LT)


def last_time(time):
    return lax.rem(time + LT - 1, LT)


def load_matrix(ref, direction, time, half=None):
    rows = rows_of(time) if not isinstance(time, int) else slice(time * LX, (time + 1) * LX)

    def load(part, i, j):
        value = ref[direction, part, i, j, rows, :].astype(F32)
        return value if half is None else value[half]

    return [[tuple(load(part, i, j) for part in (0, 1)) for j in range(3)] for i in range(3)]


def load_line(ref, slot, half):
    def load(part, i, j):
        return ref[0, ((slot * 2 + part) * 3 + i) * 3 + j].astype(F32)[half]

    return [[tuple(load(part, i, j) for part in (0, 1)) for j in range(3)] for i in range(3)]


def halved(matrix, half):
    return mapped(lambda value: value[half], matrix)


def up_x(value):
    return pltpu.roll(value, LX - 1, 0)


def down_x(value):
    return pltpu.roll(value, 1, 0)


def up_y(value):
    return pltpu.roll(value, LY - 1, 1)


def down_y(value):
    return pltpu.roll(value, 1, 1)


def neighbour_link(ref, direction, step, time):
    if step == 3:
        return load_matrix(ref, direction, next_time(time))
    return mapped(up_x if step == 0 else up_y, load_matrix(ref, direction, time))


def staple_kernel(begin, level, upward, out):
    def body(step, carry):
        time = begin + step
        up_link = load_matrix(upward, 0, time)
        for slot in range(3):
            left = product(up_link, load_matrix(level, slot, step), left_dagger=True)
            direction = (0, 1, 3)[slot]
            staple = product(left, neighbour_link(upward, 0, direction, time))
            for i in range(3):
                for j in range(3):
                    for part in (0, 1):
                        out[step, ((slot * 2 + part) * 3 + i) * 3 + j] = staple[i][j][part].astype(BF16)
        return carry

    lax.fori_loop(0, out.shape[0], body, 0)


def flat_kernel(links, out, corner):
    def lower(time, carry):
        rows = rows_of(time)
        for slot, direction in enumerate((0, 1)):
            bent = product(
                load_matrix(links, direction, time), neighbour_link(links, 3, direction, time)
            )
            bent = product(load_matrix(links, 3, time), bent, left_dagger=True)
            for i in range(3):
                for j in range(3):
                    for part in (0, 1):
                        corner[slot, part, i, j, rows, :] = bent[i][j][part]
        return carry

    lax.fori_loop(0, LT, lower, 0)

    def upper(time, carry):
        for slot, direction in enumerate((0, 1)):
            far = product(
                load_matrix(links, 3, time), neighbour_link(links, direction, 3, time)
            )
            far = product(neighbour_link(links, 3, direction, time), far, right_dagger=True)
            bend = minus_adjoint(far, load_matrix(corner, slot, last_time(time)))
            link = load_matrix(links, direction, time)
            ahead = anti_product(link, bend)
            behind = anti_product(bend, link)
            move = down_x if direction == 0 else down_y
            for index in range(HALF):
                out[time, (slot + 1) * HALF + index] = ahead[index] + move(behind[index])
        link_x, link_y = load_matrix(links, 0, time), load_matrix(links, 1, time)
        over_x, over_y = mapped(up_y, link_x), mapped(up_x, link_y)
        near = product(link_x, product(link_y, over_x), left_dagger=True)
        far = product(over_x, product(link_x, over_y), right_dagger=True)
        bend = minus_adjoint(far, mapped(down_x, near))
        ahead = anti_product(link_y, bend)
        behind = anti_product(bend, link_y)
        for index in range(HALF):
            out[time, index] = -(ahead[index] + down_y(behind[index]))
        return carry

    lax.fori_loop(0, LT, upper, 0)


def neighbour_up(links, later, step):
    if step == 3:
        return load_matrix(later, 0, 0)
    return mapped(up_x if step == 0 else up_y, load_matrix(links, 2, 0))


def z_planes(links, later, above, staples, rise, edge):
    for half in HALVES:
        up_link = load_matrix(links, 2, 0, half)
        for slot, direction in enumerate((0, 1, 3)):
            far = product(up_link, load_matrix(above, slot, 0, half))
            moved = halved(neighbour_up(links, later, direction), half)
            far = product(moved, far, right_dagger=True)
            bend = minus_adjoint(far, load_line(staples, slot, half))
            link = load_matrix(links, direction, 0, half)
            for index, value in enumerate(anti_product(link, bend)):
                rise[slot * HALF + index, half, :] = value
            for index, value in enumerate(anti_product(bend, link)):
                if direction == 1:
                    rise[HALF + index, half, :] += down_y(value)
                else:
                    edge[(0 if direction == 3 else HALF) + index, half, :] = value
    for index in range(HALF):
        rise[index] += down_x(edge[HALF + index])


def coefficients(flat, rise, before, coef):
    for block in range(2):
        sign = 1.0 if block == 0 else -1.0

        def field(number):
            parts = []
            for index in range(HALF):
                if number == 0:
                    value = sign * flat[HALF + index] - rise[HALF + index]
                elif number == 1:
                    value = -sign * flat[2 * HALF + index] - rise[index]
                else:
                    value = -flat[index] - sign * (rise[2 * HALF + index] + before[index])
                parts.append(value * 0.125)
            trace = (parts[3] + parts[4] + parts[5]) * (1.0 / 3.0)
            for index in (3, 4, 5):
                parts[index] = parts[index] - trace
            return parts

        first, second, third = field(0), field(1), field(2)
        for index in range(HALF):
            coef[block, index] = third[index] if index < 3 else -third[index]
        place = HALF
        for i in range(3):
            for j in range(3):
                if i == j:
                    re, im = -first[3 + i], second[3 + i]
                else:
                    index = UPPER.index((min(i, j), max(i, j)))
                    if i < j:
                        re = second[index] - first[6 + index]
                        im = first[index] + second[6 + index]
                    else:
                        re = -second[index] - first[6 + index]
                        im = second[6 + index] - first[index]
                coef[block, place] = re
                coef[block, place + 1] = im
                place += 2


def insert_slice(coef, plain, inserted, crossed):
    for block in range(2):
        for source in range(plain.shape[0]):
            rounded = {}
            for half in HALVES:
                spinor = [
                    [
                        tuple(
                            plain[source, part, 2 * block + spin, color].astype(F32)[half]
                            for part in (0, 1)
                        )
                        for color in range(3)
                    ]
                    for spin in range(2)
                ]
                for spin in range(2):
                    for i in range(3):
                        total_re = total_im = None
                        for j in range(3):
                            v_re, v_im = spinor[1 - spin][j]
                            row, column = (i, j) if spin == 0 else (j, i)
                            place = HALF + 2 * (3 * row + column)
                            m_re, m_im = coef[block, place, half, :], coef[block, place + 1, half, :]
                            re, im = m_re * v_re, m_re * v_im
                            total_re = re if total_re is None else total_re + re
                            total_im = im if total_im is None else total_im + im
                            if spin == 0:
                                total_re = total_re - m_im * v_im
                                total_im = total_im + m_im * v_re
                            else:
                                total_re = total_re + m_im * v_im
                                total_im = total_im - m_im * v_re
                        for j in range(3):
                            v_re, v_im = spinor[spin][j]
                            if i == j:
                                m_re, m_im = coef[block, 3 + i, half, :], None
                            else:
                                index = UPPER.index((min(i, j), max(i, j)))
                                m_re = coef[block, 6 + index, half, :]
                                m_im = coef[block, index, half, :]
                            if spin == 0:
                                total_re = total_re + m_re * v_re
                                total_im = total_im + m_re * v_im
                            else:
                                total_re = total_re - m_re * v_re
                                total_im = total_im - m_re * v_im
                            if m_im is not None:
                                if (i < j) == (spin == 0):
                                    total_re = total_re - m_im * v_im
                                    total_im = total_im + m_im * v_re
                                else:
                                    total_re = total_re + m_im * v_im
                                    total_im = total_im - m_im * v_re
                        for part, total in enumerate((total_re, total_im)):
                            rounded.setdefault((spin, i, part), []).append(total)
            for spin in range(2):
                result = []
                for i in range(3):
                    kept = []
                    for part in (0, 1):
                        value = jnp.concatenate(rounded[spin, i, part], axis=0).astype(BF16)
                        inserted[source, part, 2 * block + spin, i] = value
                        kept.append(value.astype(F32))
                    result.append(kept)
                vector = [
                    [plain[source, part, 2 * block + spin, color].astype(F32) for part in (0, 1)]
                    for color in range(3)
                ]
                for a, b, c in ((0, 1, 2), (1, 2, 0), (2, 0, 1)):
                    (a_re, a_im), (b_re, b_im) = result[a], result[b]
                    (p_re, p_im), (q_re, q_im) = vector[a], vector[b]
                    crossed[0, ((source * 2) * 4 + 2 * block + spin) * 3 + c] = (
                        a_re * q_re - a_im * q_im - b_re * p_re + b_im * p_im
                    )
                    crossed[0, ((source * 2 + 1) * 4 + 2 * block + spin) * 3 + c] = (
                        a_re * q_im + a_im * q_re - b_re * p_im - b_im * p_re
                    )


def insert_kernel(begin, end, *refs):
    first, last = begin == 0, end == LT
    refs = list(refs)
    links, later, above, staples, flat, plain = refs[:6]
    refs = refs[6:]
    if not first:
        edge_in = refs.pop(0)
        if last:
            rise_zero = refs.pop(0)
        refs = refs[2:]
    inserted, crossed = refs[:2]
    refs = refs[2:]
    edge_out = rise_out = None
    if not last:
        edge_out = refs.pop(0)
        if first:
            rise_out = refs.pop(0)
    rise, edge, coef = refs
    step = pl.program_id(0)
    steps = end - begin
    slot = jnp.minimum(lax.rem(step, steps), 1) if last and first else jnp.int32(0)
    turn = lax.rem(step, 2)

    if not first:

        @pl.when(step == 0)
        def _():
            edge[1, 0:HALF] = edge_in[...]

    @pl.when(step < steps)
    def _():
        z_planes(links, later, above, staples, rise.at[slot], edge.at[turn])

    if not last:

        @pl.when(step == steps - 1)
        def _():
            edge_out[...] = edge[turn, 0:HALF]

        if first:

            @pl.when(step == 0)
            def _():
                rise_out[...] = rise[0]

    if last and not first:

        @pl.when(step == steps)
        def _():
            rise[0] = rise_zero[...]

    @pl.when(step > 0 if first else step >= 0)
    def _():
        coefficients(flat.at[0], rise.at[slot], edge.at[1 - turn], coef)
        insert_slice(coef, plain, inserted, crossed)


def project_kernel(sources, crossed, sink, wave_y, wave_x, turn, owner, out, density):
    count = sources * LT * LX

    step = pl.program_id(0)
    for inner in range(sink.shape[0] // 2):
        time = step * (sink.shape[0] // 2) + inner
        for source in range(sources):
            total_re = total_im = None
            for spin in range(4):
                for color in range(3):
                    eta = []
                    for part in (0, 1):
                        line = (((source * 2 + part) * 4) + spin) * 3 + color
                        lines = slice(line * 8, line * 8 + 8)
                        eta.append(
                            jnp.concatenate(
                                [sink[2 * inner + half, lines, :].astype(F32) for half in (0, 1)],
                                axis=0,
                            )
                        )
                    w_re = crossed[inner, ((source * 2) * 4 + spin) * 3 + color]
                    w_im = crossed[inner, ((source * 2 + 1) * 4 + spin) * 3 + color]
                    re = w_re * eta[0] - w_im * eta[1]
                    im = w_re * eta[1] + w_im * eta[0]
                    total_re = re if total_re is None else total_re + re
                    total_im = im if total_im is None else total_im + im
            place = pl.multiple_of(source * TX + time * LX, LX)
            density[pl.ds(place, LX), :] = total_re
            density[pl.ds(pl.multiple_of(count + place, LX), LX), :] = total_im

    @pl.when(step == pl.num_programs(0) - 1)
    def _():
        project(sources, wave_y, wave_x, turn, owner, out, density)


def project(sources, wave_y, wave_x, turn, owner, out, density):
    count = sources * TX
    values = density[...]
    high = values.astype(BF16)
    low = (values - high.astype(F32)).astype(BF16)
    both = functools.partial(jnp.dot, preferred_element_type=F32)
    waves = both(high, wave_y[0]) + (both(low, wave_y[0]) + both(high, wave_y[1]))
    cos_re, sin_re = waves[:count, :NMOM], waves[:count, NMOM:]
    cos_im, sin_im = waves[count:, :NMOM], waves[count:, NMOM:]
    line_re = (cos_re + sin_im).reshape(sources * LT, LX, NMOM)
    line_im = (cos_im - sin_re).reshape(sources * LT, LX, NMOM)
    cos_x, sin_x = wave_x[0][None], wave_x[1][None]
    sum_re = jnp.sum(line_re * cos_x + line_im * sin_x, axis=1)
    sum_im = jnp.sum(line_im * cos_x - line_re * sin_x, axis=1)
    cos_t, sin_t = turn[0], turn[1]
    turned = jnp.concatenate(
        [sum_re * cos_t - sum_im * sin_t, sum_re * sin_t + sum_im * cos_t], axis=1
    )
    parts = []
    for _ in range(3):
        parts.append(turned.astype(BF16))
        turned = turned - parts[-1].astype(F32)
    out[...] = both(owner[...], jnp.concatenate(parts, axis=0))


def pack_kernel(links, *refs):
    outs, upward, sems = refs[: len(PIECES)], refs[len(PIECES)], refs[-1]
    copies = []
    for index, (out, (begin, end)) in enumerate(zip(outs, PIECES)):
        rows = slice(begin * LX, end * LX)
        for part, (place, source) in enumerate(((slice(0, 2), slice(0, 2)), (slice(2, 3), slice(3, 4)))):
            copies.append(
                pltpu.make_async_copy(
                    links.at[source, :, :, :, rows], out.at[place], sems.at[2 * index + part]
                )
            )
    copies.append(pltpu.make_async_copy(links.at[2:3], upward, sems.at[2 * len(PIECES)]))
    for copy in copies:
        copy.start()
    for copy in copies:
        copy.wait()


def spread_kernel(sink, out):
    for device in range(out.shape[0]):
        piece = sink[:, :, device * LY : (device + 1) * LY].astype(F32)
        out[device] = piece.reshape(out.shape[1], LY).astype(BF16)


def params(megabytes=56):
    return pltpu.CompilerParams(vmem_limit_bytes=megabytes << 20)


def slab_block(lead, time_of):
    return pl.BlockSpec(
        tuple(lead) + (LX, LY), lambda step: (0,) * len(lead) + (time_of(step), 0)
    )


def up_block(time_of):
    return pl.BlockSpec((1, 2, 3, 3, LX, LY), lambda step: (2, 0, 0, 0, time_of(step), 0))


def whole(count):
    return [pl.BlockSpec(memory_space=pltpu.VMEM)] * count


def cost(flops, moved):
    return pl.CostEstimate(flops=flops, bytes_accessed=moved, transcendentals=0)


def momenta():
    index = np.arange(NMOM)
    return index % 4 - 1, index // 4 % 4 - 1, index // 16 - NMOM // 32


def wave_tables():
    wave_x, wave_y, _ = momenta()
    angle_y = 2.0 * np.pi * ((wave_y[None, :] * np.arange(LY)[:, None]) % LY) / LY
    table = np.concatenate([np.cos(angle_y), np.sin(angle_y)], axis=1)
    high = table.astype(jnp.bfloat16)
    low = (table - high.astype(np.float64)).astype(jnp.bfloat16)
    angle_x = 2.0 * np.pi * ((wave_x[None, :] * np.arange(LX)[:, None]) % LX) / LX
    along_x = np.stack([np.cos(angle_x), np.sin(angle_x)]).astype(np.float32)
    return np.stack([high, low]), along_x


def turn_table(source_place, z_position, extent_z):
    wave_x, wave_y, wave_z = (jnp.asarray(w, jnp.int32)[None, :] for w in momenta())
    fraction = (
        (wave_x * source_place[:, 0:1] % LX).astype(F32) / LX
        + (wave_y * source_place[:, 1:2] % LY).astype(F32) / LY
        + (wave_z * (source_place[:, 2:3] - z_position) % extent_z).astype(F32) / extent_z
    )
    angle = 2.0 * math.pi * fraction
    scale = OUTPUT_SCALE / math.sqrt(LX * LY * extent_z)
    table = jnp.stack([jnp.cos(angle), jnp.sin(angle)]) * scale
    return jnp.repeat(table, LT, axis=1)


def owner_table(source_time, pair_source, pair_separation, pair_owner, row_count):
    sources = source_time.shape[0]
    pairs = pair_source.shape[0]
    hits = pair_source[:, None] == jnp.arange(sources, dtype=jnp.int32)[None, :]
    start = jnp.sum(jnp.where(hits, source_time[None, :], 0), axis=1)
    chosen = pair_source * LT + (start + pair_separation) % LT
    picks = chosen[:, None] == jnp.arange(sources * LT, dtype=jnp.int32)[None, :]
    owner = pair_owner[:, 0]
    number = jnp.arange(pairs, dtype=jnp.int32)
    earlier = (owner[:, None] == owner[None, :]) & (number[None, :] < number[:, None])
    target = owner * PADDED + jnp.sum(earlier.astype(jnp.int32), axis=1)
    rows = jnp.arange(row_count, dtype=jnp.int32)[:, None] == target[None, :]
    table = jnp.dot(rows.astype(BF16), picks.astype(BF16), preferred_element_type=F32)
    return jnp.concatenate([table.astype(BF16)] * 3, axis=1)


def on_device(
    gauge_links,
    propagators,
    sink_cotangent,
    source_time,
    source_place,
    pair_source,
    pair_separation,
    pair_owner,
):
    devices = lax.axis_size("space")
    assert gauge_links.shape[5] == LY
    sources = propagators.shape[0]
    lines = sources * 2 * 4 * 3
    slab = TX // devices
    site = (TX, LY)

    matrices = (3, 2, 3, 3)
    *levels, upward = pl.pallas_call(
        pack_kernel,
        out_shape=[
            jax.ShapeDtypeStruct(matrices + ((end - begin) * LX, LY), BF16)
            for begin, end in PIECES
        ]
        + [jax.ShapeDtypeStruct((1, 2, 3, 3) + site, BF16)],
        in_specs=[pl.BlockSpec(memory_space=pl.ANY)],
        out_specs=whole(len(PIECES) + 1),
        scratch_shapes=[pltpu.SemaphoreType.DMA((2 * len(PIECES) + 1,))],
        compiler_params=params(50),
        cost_estimate=cost(1000, 1000),
        name="pack",
    )(gauge_links)
    def piece_staples(index):
        begin, end = PIECES[index]
        return pl.pallas_call(
            functools.partial(staple_kernel, begin),
            out_shape=jax.ShapeDtypeStruct((end - begin, 54, LX, LY), BF16),
            in_specs=whole(2),
            out_specs=whole(1)[0],
            compiler_params=params(12),
            cost_estimate=cost(1000, 1000),
            name="staples",
        )(levels[index], upward)

    above = [from_behind(level, -1) for level in levels]
    staples = [from_behind(piece_staples(0), 1)]

    if slab == 8:
        spread = pl.pallas_call(
            spread_kernel,
            out_shape=jax.ShapeDtypeStruct((devices, lines * slab, LY), BF16),
            grid=(4,),
            in_specs=[pl.BlockSpec((lines, slab, devices // 4 * LY), lambda step: (0, 0, step))],
            out_specs=pl.BlockSpec((devices // 4, lines * slab, LY), lambda step: (step, 0, 0)),
            compiler_params=params(8),
            cost_estimate=cost(1000, 1000),
            name="spread",
        )(sink_cotangent.reshape(lines, slab, devices * LY))
    else:
        spread = (
            sink_cotangent.reshape(lines, slab, devices, LY)
            .transpose(2, 0, 1, 3)
            .reshape(devices, lines * slab, LY)
        )
    sink = lax.all_to_all(spread, "space", split_axis=0, concat_axis=0, tiled=True)
    if slab != 8:
        sink = (
            sink.reshape(TX // 8, 8 // slab, lines, slab, LY)
            .transpose(0, 2, 1, 3, 4)
            .reshape(TX // 8, lines * 8, LY)
        )

    staples += [from_behind(piece_staples(index), 1) for index in range(1, len(PIECES))]

    flat = pl.pallas_call(
        flat_kernel,
        out_shape=jax.ShapeDtypeStruct((LT, 3 * HALF, LX, LY), F32),
        in_specs=whole(1),
        out_specs=whole(1)[0],
        scratch_shapes=[pltpu.VMEM((2, 2, 3, 3) + site, F32)],
        compiler_params=params(),
        cost_estimate=cost(1000, 1000),
        name="flat_planes",
    )(gauge_links)

    spinors = propagators.shape[:4]

    inserted = crossed = edge = rise_zero = None
    for index, (begin, end) in enumerate(PIECES):
        first, last = begin == 0, end == LT

        def now(step):
            return lax.rem(begin + step, LT)

        def own(step):
            return jnp.minimum(step, end - begin - 1)

        def later(step):
            return lax.rem(begin + step + 1, LT)

        def written(step):
            return lax.rem(begin + (jnp.maximum(step, 1) if first else step), LT)

        operands = [gauge_links, gauge_links, above[index], staples[index], flat, propagators]
        specs = [
            slab_block((4, 2, 3, 3), now),
            up_block(later),
            slab_block(matrices, own),
            pl.BlockSpec((1, 54, LX, LY), lambda step: (own(step), 0, 0, 0)),
            pl.BlockSpec((1, 3 * HALF, LX, LY), lambda step: (now(step), 0, 0, 0)),
            slab_block(spinors, now),
        ]
        shapes = [
            jax.ShapeDtypeStruct(propagators.shape, BF16),
            jax.ShapeDtypeStruct((LT, lines, LX, LY), F32),
        ]
        out_specs = [
            slab_block(spinors, written),
            pl.BlockSpec((1, lines, LX, LY), lambda step: (written(step), 0, 0, 0)),
        ]
        aliases = {}
        if not first:
            operands.append(edge)
            specs += whole(1)
            if last:
                operands.append(rise_zero)
                specs += whole(1)
            aliases = {len(operands): 0, len(operands) + 1: 1}
            operands += [inserted, crossed]
            specs += [pl.BlockSpec(memory_space=pl.ANY)] * 2
        if not last:
            shapes.append(jax.ShapeDtypeStruct((HALF, LX, LY), F32))
            out_specs += whole(1)
            if first:
                shapes.append(jax.ShapeDtypeStruct((3 * HALF, LX, LY), F32))
                out_specs += whole(1)
        results = pl.pallas_call(
            functools.partial(insert_kernel, begin, end),
            grid=(end - begin + last,),
            out_shape=shapes,
            in_specs=specs,
            out_specs=out_specs,
            input_output_aliases=aliases,
            scratch_shapes=[
                pltpu.VMEM((2, 3 * HALF, LX, LY), F32),
                pltpu.VMEM((2, 2 * HALF, LX, LY), F32),
                pltpu.VMEM((2, HALF + 18, LX, LY), F32),
            ],
            compiler_params=params(),
            cost_estimate=cost(8 * 10**10 if first else 1000, 1000),
            name="insertion",
        )(*operands)
        inserted, crossed = results[:2]
        if not last:
            edge = results[2]
            if first:
                rise_zero = results[3]

    table_y, table_x = wave_tables()
    turn = turn_table(source_place, lax.axis_index("space"), devices)
    owner = owner_table(
        source_time, pair_source, pair_separation, pair_owner, devices * PADDED
    )
    steps = 2
    rows = pl.pallas_call(
        functools.partial(project_kernel, sources),
        grid=(steps,),
        out_shape=jax.ShapeDtypeStruct((devices * PADDED, 2 * NMOM), F32),
        in_specs=[
            pl.BlockSpec((LT // steps, lines, LX, LY), lambda step: (step, 0, 0, 0)),
            pl.BlockSpec((TX // 8 // steps, lines * 8, LY), lambda step: (step, 0, 0)),
        ]
        + whole(4),
        out_specs=whole(1)[0],
        scratch_shapes=[pltpu.VMEM((2 * sources * TX, LY), F32)],
        compiler_params=params(),
        cost_estimate=cost(1000, 1000),
        name="projection",
    )(crossed, sink, jnp.asarray(table_y), jnp.asarray(table_x), turn, owner)
    parts = lax.all_to_all(
        rows.reshape(devices, PADDED, 2 * NMOM), "space", split_axis=0, concat_axis=0, tiled=True
    )
    return inserted, jnp.sum(parts[:, :SLOTS], axis=0)


def solution(mesh):
    placed = (
        P("grp", None, None, None, None, "space"),
        P("grp", None, None, None, None, "space"),
        P("grp", None, None, None, "space", None),
        P("grp"),
        P("grp", None),
        P("grp"),
        P("grp"),
        P("grp", None),
    )
    return jax.shard_map(
        on_device,
        mesh=mesh,
        in_specs=placed,
        out_specs=(P("grp", None, None, None, None, "space"), P(("grp", "space"), None)),
        check_vma=False,
    )
```

```python
import functools
import math

import jax
import jax.numpy as jnp
import numpy as np
from jax import lax
from jax.experimental import pallas as pl
from jax.experimental.pallas import tpu as pltpu
from jax.sharding import PartitionSpec as P

LT = 8
LX = 16
LY = 128
TX = LT * LX
NMOM = 128
SLOTS = 4
OUTPUT_SCALE = 0.1
F32 = jnp.float32
BF16 = jnp.bfloat16
PIECES = ((0, 5), (5, 8))
PADDED = 8
UPPER = ((0, 1), (0, 2), (1, 2))
SYMMETRIC = ((0, 0), (1, 1), (2, 2), (0, 1), (0, 2), (1, 2))
HALVES = (slice(0, 16),)
HALF = len(UPPER) + len(SYMMETRIC)


def from_behind(block, distance):
    count = lax.axis_size("space")
    return lax.ppermute(block, "space", [((i - distance) % count, i) for i in range(count)])


def entry(left, right, row, col, left_dagger, right_dagger, part):
    total = None
    for inner in range(3):
        a_re, a_im = left[inner][row] if left_dagger else left[row][inner]
        b_re, b_im = right[col][inner] if right_dagger else right[inner][col]
        if part == 0:
            first, second = a_re * b_re, a_im * b_im
            negative = left_dagger == right_dagger
        elif left_dagger:
            first, second = a_re * b_im, a_im * b_re
            negative = True
        else:
            first, second = a_im * b_re, a_re * b_im
            negative = right_dagger
        total = first if total is None else total + first
        total = total - second if negative else total + second
    return total


def product(left, right, left_dagger=False, right_dagger=False):
    return [
        [
            tuple(entry(left, right, i, j, left_dagger, right_dagger, part) for part in (0, 1))
            for j in range(3)
        ]
        for i in range(3)
    ]


def anti_product(left, right):
    kept = []
    for i, j in UPPER:
        kept.append(entry(left, right, i, j, False, False, 0) - entry(left, right, j, i, False, False, 0))
    for i, j in SYMMETRIC:
        value = entry(left, right, i, j, False, False, 1)
        kept.append(value + (value if i == j else entry(left, right, j, i, False, False, 1)))
    return kept


def minus_adjoint(left, right):
    return [
        [
            (left[i][j][0] - right[j][i][0], left[i][j][1] + right[j][i][1])
            for j in range(3)
        ]
        for i in range(3)
    ]


def mapped(function, matrix):
    return [[tuple(function(part) for part in item) for item in row] for row in matrix]


def rows_of(time):
    return pl.ds(pl.multiple_of(time * LX, LX), LX)


def next_time(time):
    return lax.rem(time + 1, LT)


def last_time(time):
    return lax.rem(time + LT - 1, LT)


def load_matrix(ref, direction, time, half=None):
    rows = rows_of(time) if not isinstance(time, int) else slice(time * LX, (time + 1) * LX)

    def load(part, i, j):
        value = ref[direction, part, i, j, rows, :].astype(F32)
        return value if half is None else value[half]

    return [[tuple(load(part, i, j) for part in (0, 1)) for j in range(3)] for i in range(3)]


def load_line(ref, slot, half):
    def load(part, i, j):
        return ref[0, ((slot * 2 + part) * 3 + i) * 3 + j].astype(F32)[half]

    return [[tuple(load(part, i, j) for part in (0, 1)) for j in range(3)] for i in range(3)]


def halved(matrix, half):
    return mapped(lambda value: value[half], matrix)


def up_x(value):
    return pltpu.roll(value, LX - 1, 0)


def down_x(value):
    return pltpu.roll(value, 1, 0)


def up_y(value):
    return pltpu.roll(value, LY - 1, 1)


def down_y(value):
    return pltpu.roll(value, 1, 1)


def neighbour_link(ref, direction, step, time):
    if step == 3:
        return load_matrix(ref, direction, next_time(time))
    return mapped(up_x if step == 0 else up_y, load_matrix(ref, direction, time))


def staple_kernel(begin, level, upward, out):
    def body(step, carry):
        time = begin + step
        up_link = load_matrix(upward, 0, time)
        for slot in range(3):
            left = product(up_link, load_matrix(level, slot, step), left_dagger=True)
            direction = (0, 1, 3)[slot]
            staple = product(left, neighbour_link(upward, 0, direction, time))
            for i in range(3):
                for j in range(3):
                    for part in (0, 1):
                        out[step, ((slot * 2 + part) * 3 + i) * 3 + j] = staple[i][j][part].astype(BF16)
        return carry

    lax.fori_loop(0, out.shape[0], body, 0)


def flat_kernel(links, out, corner):
    def lower(time, carry):
        rows = rows_of(time)
        for slot, direction in enumerate((0, 1)):
            bent = product(
                load_matrix(links, direction, time), neighbour_link(links, 3, direction, time)
            )
            bent = product(load_matrix(links, 3, time), bent, left_dagger=True)
            for i in range(3):
                for j in range(3):
                    for part in (0, 1):
                        corner[slot, part, i, j, rows, :] = bent[i][j][part]
        return carry

    lax.fori_loop(0, LT, lower, 0)

    def upper(time, carry):
        for slot, direction in enumerate((0, 1)):
            far = product(
                load_matrix(links, 3, time), neighbour_link(links, direction, 3, time)
            )
            far = product(neighbour_link(links, 3, direction, time), far, right_dagger=True)
            bend = minus_adjoint(far, load_matrix(corner, slot, last_time(time)))
            link = load_matrix(links, direction, time)
            ahead = anti_product(link, bend)
            behind = anti_product(bend, link)
            move = down_x if direction == 0 else down_y
            for index in range(HALF):
                out[time, (slot + 1) * HALF + index] = ahead[index] + move(behind[index])
        link_x, link_y = load_matrix(links, 0, time), load_matrix(links, 1, time)
        over_x, over_y = mapped(up_y, link_x), mapped(up_x, link_y)
        near = product(link_x, product(link_y, over_x), left_dagger=True)
        far = product(over_x, product(link_x, over_y), right_dagger=True)
        bend = minus_adjoint(far, mapped(down_x, near))
        ahead = anti_product(link_y, bend)
        behind = anti_product(bend, link_y)
        for index in range(HALF):
            out[time, index] = -(ahead[index] + down_y(behind[index]))
        return carry

    lax.fori_loop(0, LT, upper, 0)


def neighbour_up(links, later, step):
    if step == 3:
        return load_matrix(later, 0, 0)
    return mapped(up_x if step == 0 else up_y, load_matrix(links, 2, 0))


def z_planes(links, later, above, staples, rise, edge):
    for half in HALVES:
        up_link = load_matrix(links, 2, 0, half)
        for slot, direction in enumerate((0, 1, 3)):
            far = product(up_link, load_matrix(above, slot, 0, half))
            moved = halved(neighbour_up(links, later, direction), half)
            far = product(moved, far, right_dagger=True)
            bend = minus_adjoint(far, load_line(staples, slot, half))
            link = load_matrix(links, direction, 0, half)
            for index, value in enumerate(anti_product(link, bend)):
                rise[slot * HALF + index, half, :] = value
            for index, value in enumerate(anti_product(bend, link)):
                if direction == 1:
                    rise[HALF + index, half, :] += down_y(value)
                else:
                    edge[(0 if direction == 3 else HALF) + index, half, :] = value
    for index in range(HALF):
        rise[index] += down_x(edge[HALF + index])


def coefficients(flat, rise, before, coef):
    for block in range(2):
        sign = 1.0 if block == 0 else -1.0

        def field(number):
            parts = []
            for index in range(HALF):
                if number == 0:
                    value = sign * flat[HALF + index] - rise[HALF + index]
                elif number == 1:
                    value = -sign * flat[2 * HALF + index] - rise[index]
                else:
                    value = -flat[index] - sign * (rise[2 * HALF + index] + before[index])
                parts.append(value * 0.125)
            trace = (parts[3] + parts[4] + parts[5]) * (1.0 / 3.0)
            for index in (3, 4, 5):
                parts[index] = parts[index] - trace
            return parts

        first, second, third = field(0), field(1), field(2)
        for index in range(HALF):
            coef[block, index] = third[index] if index < 3 else -third[index]
        place = HALF
        for i in range(3):
            for j in range(3):
                if i == j:
                    re, im = -first[3 + i], second[3 + i]
                else:
                    index = UPPER.index((min(i, j), max(i, j)))
                    if i < j:
                        re = second[index] - first[6 + index]
                        im = first[index] + second[6 + index]
                    else:
                        re = -second[index] - first[6 + index]
                        im = second[6 + index] - first[index]
                coef[block, place] = re
                coef[block, place + 1] = im
                place += 2


def insert_slice(coef, plain, inserted, crossed):
    for block in range(2):
        for source in range(plain.shape[0]):
            rounded = {}
            whole_spinor = [
                [
                    tuple(
                        plain[source, part, 2 * block + spin, color].astype(F32) for part in (0, 1)
                    )
                    for color in range(3)
                ]
                for spin in range(2)
            ]
            for half in HALVES:
                spinor = [
                    [tuple(part[half] for part in item) for item in row] for row in whole_spinor
                ]
                for spin in range(2):
                    for i in range(3):
                        total_re = total_im = None
                        for j in range(3):
                            v_re, v_im = spinor[1 - spin][j]
                            row, column = (i, j) if spin == 0 else (j, i)
                            place = HALF + 2 * (3 * row + column)
                            m_re, m_im = coef[block, place, half, :], coef[block, place + 1, half, :]
                            re, im = m_re * v_re, m_re * v_im
                            total_re = re if total_re is None else total_re + re
                            total_im = im if total_im is None else total_im + im
                            if spin == 0:
                                total_re = total_re - m_im * v_im
                                total_im = total_im + m_im * v_re
                            else:
                                total_re = total_re + m_im * v_im
                                total_im = total_im - m_im * v_re
                        for j in range(3):
                            v_re, v_im = spinor[spin][j]
                            if i == j:
                                m_re, m_im = coef[block, 3 + i, half, :], None
                            else:
                                index = UPPER.index((min(i, j), max(i, j)))
                                m_re = coef[block, 6 + index, half, :]
                                m_im = coef[block, index, half, :]
                            if spin == 0:
                                total_re = total_re + m_re * v_re
                                total_im = total_im + m_re * v_im
                            else:
                                total_re = total_re - m_re * v_re
                                total_im = total_im - m_re * v_im
                            if m_im is not None:
                                if (i < j) == (spin == 0):
                                    total_re = total_re - m_im * v_im
                                    total_im = total_im + m_im * v_re
                                else:
                                    total_re = total_re + m_im * v_im
                                    total_im = total_im - m_im * v_re
                        for part, total in enumerate((total_re, total_im)):
                            rounded.setdefault((spin, i, part), []).append(total)
            for spin in range(2):
                result = []
                for i in range(3):
                    kept = []
                    for part in (0, 1):
                        value = jnp.concatenate(rounded[spin, i, part], axis=0).astype(BF16)
                        inserted[source, part, 2 * block + spin, i] = value
                        kept.append(value.astype(F32))
                    result.append(kept)
                vector = whole_spinor[spin]
                for a, b, c in ((0, 1, 2), (1, 2, 0), (2, 0, 1)):
                    (a_re, a_im), (b_re, b_im) = result[a], result[b]
                    (p_re, p_im), (q_re, q_im) = vector[a], vector[b]
                    crossed[0, ((source * 2) * 4 + 2 * block + spin) * 3 + c] = (
                        a_re * q_re - a_im * q_im - b_re * p_re + b_im * p_im
                    )
                    crossed[0, ((source * 2 + 1) * 4 + 2 * block + spin) * 3 + c] = (
                        a_re * q_im + a_im * q_re - b_re * p_im - b_im * p_re
                    )


def insert_kernel(begin, end, *refs):
    first, last = begin == 0, end == LT
    refs = list(refs)
    links, later, above, staples, flat, plain = refs[:6]
    refs = refs[6:]
    if not first:
        edge_in = refs.pop(0)
        if last:
            rise_zero = refs.pop(0)
        refs = refs[2:]
    inserted, crossed = refs[:2]
    refs = refs[2:]
    edge_out = rise_out = None
    if not last:
        edge_out = refs.pop(0)
        if first:
            rise_out = refs.pop(0)
    rise, edge, coef = refs
    step = pl.program_id(0)
    steps = end - begin
    slot = jnp.minimum(lax.rem(step, steps), 1) if last and first else jnp.int32(0)
    turn = lax.rem(step, 2)

    if not first:

        @pl.when(step == 0)
        def _():
            edge[1, 0:HALF] = edge_in[...]

    @pl.when(step < steps)
    def _():
        z_planes(links, later, above, staples, rise.at[slot], edge.at[turn])

    if not last:

        @pl.when(step == steps - 1)
        def _():
            edge_out[...] = edge[turn, 0:HALF]

        if first:

            @pl.when(step == 0)
            def _():
                rise_out[...] = rise[0]

    if last and not first:

        @pl.when(step == steps)
        def _():
            rise[0] = rise_zero[...]

    @pl.when(step > 0 if first else step >= 0)
    def _():
        coefficients(flat.at[0], rise.at[slot], edge.at[1 - turn], coef)
        insert_slice(coef, plain, inserted, crossed)


def project_kernel(sources, crossed, sink, wave_y, wave_x, turn, owner, out, density):
    count = sources * LT * LX

    step = pl.program_id(0)
    for inner in range(sink.shape[0] // 2):
        time = step * (sink.shape[0] // 2) + inner
        for source in range(sources):
            total_re = total_im = None
            for spin in range(4):
                for color in range(3):
                    eta = []
                    for part in (0, 1):
                        line = (((source * 2 + part) * 4) + spin) * 3 + color
                        lines = slice(line * 8, line * 8 + 8)
                        eta.append(
                            jnp.concatenate(
                                [sink[2 * inner + half, lines, :].astype(F32) for half in (0, 1)],
                                axis=0,
                            )
                        )
                    w_re = crossed[inner, ((source * 2) * 4 + spin) * 3 + color]
                    w_im = crossed[inner, ((source * 2 + 1) * 4 + spin) * 3 + color]
                    re = w_re * eta[0] - w_im * eta[1]
                    im = w_re * eta[1] + w_im * eta[0]
                    total_re = re if total_re is None else total_re + re
                    total_im = im if total_im is None else total_im + im
            place = pl.multiple_of(source * TX + time * LX, LX)
            density[pl.ds(place, LX), :] = total_re
            density[pl.ds(pl.multiple_of(count + place, LX), LX), :] = total_im

    @pl.when(step == pl.num_programs(0) - 1)
    def _():
        project(sources, wave_y, wave_x, turn, owner, out, density)


def project(sources, wave_y, wave_x, turn, owner, out, density):
    count = sources * TX
    values = density[...]
    high = values.astype(BF16)
    low = (values - high.astype(F32)).astype(BF16)
    both = functools.partial(jnp.dot, preferred_element_type=F32)
    waves = both(high, wave_y[0]) + (both(low, wave_y[0]) + both(high, wave_y[1]))
    cos_re, sin_re = waves[:count, :NMOM], waves[:count, NMOM:]
    cos_im, sin_im = waves[count:, :NMOM], waves[count:, NMOM:]
    line_re = (cos_re + sin_im).reshape(sources * LT, LX, NMOM)
    line_im = (cos_im - sin_re).reshape(sources * LT, LX, NMOM)
    cos_x, sin_x = wave_x[0][None], wave_x[1][None]
    sum_re = jnp.sum(line_re * cos_x + line_im * sin_x, axis=1)
    sum_im = jnp.sum(line_im * cos_x - line_re * sin_x, axis=1)
    cos_t, sin_t = turn[0], turn[1]
    turned = jnp.concatenate(
        [sum_re * cos_t - sum_im * sin_t, sum_re * sin_t + sum_im * cos_t], axis=1
    )
    parts = []
    for _ in range(3):
        parts.append(turned.astype(BF16))
        turned = turned - parts[-1].astype(F32)
    out[...] = both(owner[...], jnp.concatenate(parts, axis=0))


def pack_kernel(links, *refs):
    outs, upward, sems = refs[: len(PIECES)], refs[len(PIECES)], refs[-1]
    copies = []
    for index, (out, (begin, end)) in enumerate(zip(outs, PIECES)):
        rows = slice(begin * LX, end * LX)
        for part, (place, source) in enumerate(((slice(0, 2), slice(0, 2)), (slice(2, 3), slice(3, 4)))):
            copies.append(
                pltpu.make_async_copy(
                    links.at[source, :, :, :, rows], out.at[place], sems.at[2 * index + part]
                )
            )
    copies.append(pltpu.make_async_copy(links.at[2:3], upward, sems.at[2 * len(PIECES)]))
    for copy in copies:
        copy.start()
    for copy in copies:
        copy.wait()


def spread_kernel(sink, out):
    for device in range(out.shape[0]):
        piece = sink[:, :, device * LY : (device + 1) * LY].astype(F32)
        out[device] = piece.reshape(out.shape[1], LY).astype(BF16)


def params(megabytes=56):
    return pltpu.CompilerParams(vmem_limit_bytes=megabytes << 20)


def slab_block(lead, time_of):
    return pl.BlockSpec(
        tuple(lead) + (LX, LY), lambda step: (0,) * len(lead) + (time_of(step), 0)
    )


def up_block(time_of):
    return pl.BlockSpec((1, 2, 3, 3, LX, LY), lambda step: (2, 0, 0, 0, time_of(step), 0))


def whole(count):
    return [pl.BlockSpec(memory_space=pltpu.VMEM)] * count


def cost(flops, moved):
    return pl.CostEstimate(flops=flops, bytes_accessed=moved, transcendentals=0)


def momenta():
    index = np.arange(NMOM)
    return index % 4 - 1, index // 4 % 4 - 1, index // 16 - NMOM // 32


def wave_tables():
    wave_x, wave_y, _ = momenta()
    angle_y = 2.0 * np.pi * ((wave_y[None, :] * np.arange(LY)[:, None]) % LY) / LY
    table = np.concatenate([np.cos(angle_y), np.sin(angle_y)], axis=1)
    high = table.astype(jnp.bfloat16)
    low = (table - high.astype(np.float64)).astype(jnp.bfloat16)
    angle_x = 2.0 * np.pi * ((wave_x[None, :] * np.arange(LX)[:, None]) % LX) / LX
    along_x = np.stack([np.cos(angle_x), np.sin(angle_x)]).astype(np.float32)
    return np.stack([high, low]), along_x


def turn_table(source_place, z_position, extent_z):
    wave_x, wave_y, wave_z = (jnp.asarray(w, jnp.int32)[None, :] for w in momenta())
    fraction = (
        (wave_x * source_place[:, 0:1] % LX).astype(F32) / LX
        + (wave_y * source_place[:, 1:2] % LY).astype(F32) / LY
        + (wave_z * (source_place[:, 2:3] - z_position) % extent_z).astype(F32) / extent_z
    )
    angle = 2.0 * math.pi * fraction
    scale = OUTPUT_SCALE / math.sqrt(LX * LY * extent_z)
    table = jnp.stack([jnp.cos(angle), jnp.sin(angle)]) * scale
    return jnp.repeat(table, LT, axis=1)


def owner_table(source_time, pair_source, pair_separation, pair_owner, row_count):
    sources = source_time.shape[0]
    pairs = pair_source.shape[0]
    hits = pair_source[:, None] == jnp.arange(sources, dtype=jnp.int32)[None, :]
    start = jnp.sum(jnp.where(hits, source_time[None, :], 0), axis=1)
    chosen = pair_source * LT + (start + pair_separation) % LT
    picks = chosen[:, None] == jnp.arange(sources * LT, dtype=jnp.int32)[None, :]
    owner = pair_owner[:, 0]
    number = jnp.arange(pairs, dtype=jnp.int32)
    earlier = (owner[:, None] == owner[None, :]) & (number[None, :] < number[:, None])
    target = owner * PADDED + jnp.sum(earlier.astype(jnp.int32), axis=1)
    rows = jnp.arange(row_count, dtype=jnp.int32)[:, None] == target[None, :]
    table = jnp.dot(rows.astype(BF16), picks.astype(BF16), preferred_element_type=F32)
    return jnp.concatenate([table.astype(BF16)] * 3, axis=1)


def on_device(
    gauge_links,
    propagators,
    sink_cotangent,
    source_time,
    source_place,
    pair_source,
    pair_separation,
    pair_owner,
):
    devices = lax.axis_size("space")
    assert gauge_links.shape[5] == LY
    sources = propagators.shape[0]
    lines = sources * 2 * 4 * 3
    slab = TX // devices
    site = (TX, LY)

    matrices = (3, 2, 3, 3)
    *levels, upward = pl.pallas_call(
        pack_kernel,
        out_shape=[
            jax.ShapeDtypeStruct(matrices + ((end - begin) * LX, LY), BF16)
            for begin, end in PIECES
        ]
        + [jax.ShapeDtypeStruct((1, 2, 3, 3) + site, BF16)],
        in_specs=[pl.BlockSpec(memory_space=pl.ANY)],
        out_specs=whole(len(PIECES) + 1),
        scratch_shapes=[pltpu.SemaphoreType.DMA((2 * len(PIECES) + 1,))],
        compiler_params=params(50),
        cost_estimate=cost(1000, 1000),
        name="pack",
    )(gauge_links)
    def piece_staples(index):
        begin, end = PIECES[index]
        return pl.pallas_call(
            functools.partial(staple_kernel, begin),
            out_shape=jax.ShapeDtypeStruct((end - begin, 54, LX, LY), BF16),
            in_specs=whole(2),
            out_specs=whole(1)[0],
            compiler_params=params(12),
            cost_estimate=cost(1000, 1000),
            name="staples",
        )(levels[index], upward)

    above = [from_behind(level, -1) for level in levels]
    staples = [from_behind(piece_staples(0), 1)]

    if slab == 8:
        spread = pl.pallas_call(
            spread_kernel,
            out_shape=jax.ShapeDtypeStruct((devices, lines * slab, LY), BF16),
            grid=(4,),
            in_specs=[pl.BlockSpec((lines, slab, devices // 4 * LY), lambda step: (0, 0, step))],
            out_specs=pl.BlockSpec((devices // 4, lines * slab, LY), lambda step: (step, 0, 0)),
            compiler_params=params(8),
            cost_estimate=cost(1000, 1000),
            name="spread",
        )(sink_cotangent.reshape(lines, slab, devices * LY))
    else:
        spread = (
            sink_cotangent.reshape(lines, slab, devices, LY)
            .transpose(2, 0, 1, 3)
            .reshape(devices, lines * slab, LY)
        )
    sink = lax.all_to_all(spread, "space", split_axis=0, concat_axis=0, tiled=True)
    if slab != 8:
        sink = (
            sink.reshape(TX // 8, 8 // slab, lines, slab, LY)
            .transpose(0, 2, 1, 3, 4)
            .reshape(TX // 8, lines * 8, LY)
        )

    staples += [from_behind(piece_staples(index), 1) for index in range(1, len(PIECES))]

    flat = pl.pallas_call(
        flat_kernel,
        out_shape=jax.ShapeDtypeStruct((LT, 3 * HALF, LX, LY), F32),
        in_specs=whole(1),
        out_specs=whole(1)[0],
        scratch_shapes=[pltpu.VMEM((2, 2, 3, 3) + site, F32)],
        compiler_params=params(),
        cost_estimate=cost(1000, 1000),
        name="flat_planes",
    )(gauge_links)

    spinors = propagators.shape[:4]

    inserted = crossed = edge = rise_zero = None
    for index, (begin, end) in enumerate(PIECES):
        first, last = begin == 0, end == LT

        def now(step):
            return begin + own(step)

        def own(step):
            return jnp.minimum(step, end - begin - 1)

        def later(step):
            return lax.rem(begin + own(step) + 1, LT)

        def written(step):
            return lax.rem(begin + (jnp.maximum(step, 1) if first else step), LT)

        operands = [gauge_links, gauge_links, above[index], staples[index], flat, propagators]
        specs = [
            slab_block((4, 2, 3, 3), now),
            up_block(later),
            slab_block(matrices, own),
            pl.BlockSpec((1, 54, LX, LY), lambda step: (own(step), 0, 0, 0)),
            pl.BlockSpec((1, 3 * HALF, LX, LY), lambda step: (written(step), 0, 0, 0)),
            slab_block(spinors, written),
        ]
        shapes = [
            jax.ShapeDtypeStruct(propagators.shape, BF16),
            jax.ShapeDtypeStruct((LT, lines, LX, LY), F32),
        ]
        out_specs = [
            slab_block(spinors, written),
            pl.BlockSpec((1, lines, LX, LY), lambda step: (written(step), 0, 0, 0)),
        ]
        aliases = {}
        if not first:
            operands.append(edge)
            specs += whole(1)
            if last:
                operands.append(rise_zero)
                specs += whole(1)
            aliases = {len(operands): 0, len(operands) + 1: 1}
            operands += [inserted, crossed]
            specs += [pl.BlockSpec(memory_space=pl.ANY)] * 2
        if not last:
            shapes.append(jax.ShapeDtypeStruct((HALF, LX, LY), F32))
            out_specs += whole(1)
            if first:
                shapes.append(jax.ShapeDtypeStruct((3 * HALF, LX, LY), F32))
                out_specs += whole(1)
        results = pl.pallas_call(
            functools.partial(insert_kernel, begin, end),
            grid=(end - begin + last,),
            out_shape=shapes,
            in_specs=specs,
            out_specs=out_specs,
            input_output_aliases=aliases,
            scratch_shapes=[
                pltpu.VMEM((2, 3 * HALF, LX, LY), F32),
                pltpu.VMEM((2, 2 * HALF, LX, LY), F32),
                pltpu.VMEM((2, HALF + 18, LX, LY), F32),
            ],
            compiler_params=params(),
            cost_estimate=cost(8 * 10**10 if first else 1000, 1000),
            name="insertion",
        )(*operands)
        inserted, crossed = results[:2]
        if not last:
            edge = results[2]
            if first:
                rise_zero = results[3]

    table_y, table_x = wave_tables()
    turn = turn_table(source_place, lax.axis_index("space"), devices)
    owner = owner_table(
        source_time, pair_source, pair_separation, pair_owner, devices * PADDED
    )
    steps = 2
    rows = pl.pallas_call(
        functools.partial(project_kernel, sources),
        grid=(steps,),
        out_shape=jax.ShapeDtypeStruct((devices * PADDED, 2 * NMOM), F32),
        in_specs=[
            pl.BlockSpec((LT // steps, lines, LX, LY), lambda step: (step, 0, 0, 0)),
            pl.BlockSpec((TX // 8 // steps, lines * 8, LY), lambda step: (step, 0, 0)),
        ]
        + whole(4),
        out_specs=whole(1)[0],
        scratch_shapes=[pltpu.VMEM((2 * sources * TX, LY), F32)],
        compiler_params=params(),
        cost_estimate=cost(1000, 1000),
        name="projection",
    )(crossed, sink, jnp.asarray(table_y), jnp.asarray(table_x), turn, owner)
    parts = lax.all_to_all(
        rows.reshape(devices, PADDED, 2 * NMOM), "space", split_axis=0, concat_axis=0, tiled=True
    )
    return inserted, jnp.sum(parts[:, :SLOTS], axis=0)


def solution(mesh):
    placed = (
        P("grp", None, None, None, None, "space"),
        P("grp", None, None, None, None, "space"),
        P("grp", None, None, None, "space", None),
        P("grp"),
        P("grp", None),
        P("grp"),
        P("grp"),
        P("grp", None),
    )
    return jax.shard_map(
        on_device,
        mesh=mesh,
        in_specs=placed,
        out_specs=(P("grp", None, None, None, None, "space"), P(("grp", "space"), None)),
        check_vma=False,
    )
```
